256 devices in a mesh: wide: 32 (over y, z), narrow: 8 (over x, core).
Axes of the slice: x: 4, y: 4, z: 8, core: 2. Of those that a mesh axis runs over, the one named last changes fastest.
Arguments:
- coefficients: float32 [3, 512, 64, 512], P(None, 'wide', 'narrow'), may hold values from 0.3 to 3
- predicted_velocity: float32 [3, 512, 64, 512], P(None, 'wide', 'narrow'), may hold values from -3 to 3
- tracers: float32 [16, 512, 64, 512], P(None, 'wide', 'narrow'), may hold values from 0.1 to 2
Outputs:
- pressure: float32 [512, 64, 512], P('wide', 'narrow')
- velocity: float32 [3, 512, 64, 512], P(None, 'wide', 'narrow')
- transported: float32 [16, 512, 64, 512], P(None, 'wide', 'narrow')
The draws below stay inside these ranges and needn't reach their ends.
All inputs are finite; a program needn't handle non-finite values.
Results may differ from the reference program's by a relative error of at most 0.0001.
Values sent between devices are 32-bit elements; how exact they have to be, the bound alone decides.
A program may use at most 192 MiB of HBM per device.

```python
import math
import jax
import jax.numpy as jnp
from jax import lax

CZ = 512
FIELDS = 16
ITERS = 3
SUBSTEPS = 2
NX = 512
NY = 64


def levels(own_key, dims, cuts, low, high):
    def one(dim, blocks):
        steps = jax.random.uniform(jax.random.fold_in(jax.random.fold_in(own_key, 6), dim), (blocks,), jnp.float32, low / len(cuts), high / len(cuts))
        return jnp.repeat(jnp.exp(steps), dims[dim] // blocks).reshape((-1,) + (1,) * (len(dims) - dim - 1))

    loudness = one(*cuts[0])
    for cut in cuts[1:]:
        loudness = loudness * one(*cut)
    return loudness


def scatter_about(own_key, extent, spread, limit, split=(), held_as=jnp.bfloat16):
    array = spread * jax.random.normal(own_key, extent, jnp.float32)
    if split:
        array = array * levels(own_key, extent, split, -0.22, 0.18)
    return jnp.clip(array, -limit, limit).astype(held_as)


def setup_inputs(seed: int = 0) -> dict:
    arg_keys = jax.random.split(jax.random.key(seed), 4)
    coefficients = jnp.clip(jnp.exp(math.log(3.0) - 2.3025851 * jax.random.uniform(arg_keys[0], (3, NX, NY, CZ), jnp.float32) ** levels(arg_keys[0], (3, NX, NY, CZ), ((1, 32), (2, 8)), -0.2, 0.2)), 0.3, 3.0)
    predicted_velocity = scatter_about(arg_keys[1], (3, NX, NY, CZ), 0.5, 3.0, ((1, 32), (2, 8)), jnp.float32)
    tracers = jnp.clip(jnp.exp(math.log(2.0) - 2.9957323 * jax.random.uniform(arg_keys[2], (FIELDS, NX, NY, CZ), jnp.float32) ** levels(arg_keys[2], (FIELDS, NX, NY, CZ), ((1, 32), (2, 8)), -0.2, 0.2)), 0.1, 2.0)
    return dict(coefficients=coefficients, predicted_velocity=predicted_velocity, tracers=tracers)


COURANT = 0.15


def lower(field, axis):
    first = jnp.zeros_like(lax.slice_in_dim(field, 0, 1, axis=axis))
    rest = lax.slice_in_dim(field, 0, field.shape[axis] - 1, axis=axis)
    return jnp.concatenate([first, rest], axis=axis)


def divergence(faces):
    return (faces[0] - lower(faces[0], 0)) + (faces[1] - lower(faces[1], 1)) + (faces[2] - lower(faces[2], 2))


def face_flux(field, coefficients):
    padded = jnp.pad(field, ((0, 1), (0, 1), (0, 1)))
    along_x = coefficients[0] * (padded[1:, :-1, :-1] - field)
    along_y = coefficients[1] * (padded[:-1, 1:, :-1] - field)
    along_z = coefficients[2] * (padded[:-1, :-1, 1:] - field)
    return jnp.stack([along_x, along_y, along_z])


def operator(field, coefficients):
    return -divergence(face_flux(field, coefficients))


def upwind_step(tracer_ext, flow_ext):
    span_a = tracer_ext.shape[1] - 2
    span_b = tracer_ext.shape[2] - 2
    inner = tracer_ext[:, 1:span_a + 1, 1:span_b + 1]
    speed = flow_ext[0, 0:span_a + 1, 1:span_b + 1]
    flux = jnp.maximum(speed, 0.0) * tracer_ext[:, 0:span_a + 1, 1:span_b + 1] + jnp.minimum(speed, 0.0) * tracer_ext[:, 1:span_a + 2, 1:span_b + 1]
    change = flux[:, 1:] - flux[:, :-1]
    speed = flow_ext[1, 1:span_a + 1, 0:span_b + 1]
    flux = jnp.maximum(speed, 0.0) * tracer_ext[:, 1:span_a + 1, 0:span_b + 1] + jnp.minimum(speed, 0.0) * tracer_ext[:, 1:span_a + 1, 1:span_b + 2]
    change = change + (flux[:, :, 1:] - flux[:, :, :-1])
    speed = flow_ext[2, 1:span_a + 1, 1:span_b + 1]
    above = jnp.concatenate([inner[..., 1:], jnp.zeros_like(inner[..., :1])], axis=3)
    flux = jnp.maximum(speed, 0.0) * inner + jnp.minimum(speed, 0.0) * above
    below = jnp.concatenate([jnp.zeros_like(flux[..., :1]), flux[..., :-1]], axis=3)
    change = change + (flux - below)
    return inner - COURANT * change


def reference(coefficients, predicted_velocity, tracers):
    rhs = -divergence(predicted_velocity)
    diag = (coefficients[0] + lower(coefficients[0], 0)) + (coefficients[1] + lower(coefficients[1], 1)) + (coefficients[2] + lower(coefficients[2], 2))
    pressure = jnp.zeros_like(rhs)
    residual = rhs
    precond = residual / diag
    direction = precond
    inner = jnp.sum(residual * precond)
    for step in range(ITERS):
        image = operator(direction, coefficients)
        alpha = inner / jnp.sum(direction * image)
        pressure = pressure + alpha * direction
        if step + 1 < ITERS:
            residual = residual - alpha * image
            precond = residual / diag
            inner_next = jnp.sum(residual * precond)
            direction = precond + (inner_next / inner) * direction
            inner = inner_next
    velocity = predicted_velocity - face_flux(pressure, coefficients)
    flow_ext = jnp.pad(velocity, ((0, 0), (1, 1), (1, 1), (0, 0)))
    current = tracers
    for sub in range(SUBSTEPS):
        current = upwind_step(jnp.pad(current, ((0, 0), (1, 1), (1, 1), (0, 0))), flow_ext)
    return pressure, velocity, current
```

```python
import functools

import jax
import jax.numpy as jnp
from jax import lax
from jax.experimental import pallas as pl
from jax.experimental.pallas import tpu as pltpu
from jax.sharding import PartitionSpec as P

MESH = pl.DeviceIdType.MESH
F32 = jnp.float32
COURANT = 0.15

PLANES = 16
CH = 4
PR = CH * 8
OWN = PLANES * PR
EDGE = PLANES * CH
TR = 16
CHUNKS = 4
PER = TR // CHUNKS
NWIDE = 32
NNARROW = 8
SHIFT = 1.0


def lane_id():
    return lax.broadcasted_iota(jnp.int32, (8, 128), 1)


def sub_id():
    return lax.broadcasted_iota(jnp.int32, (8, 128), 0)


def next_k(xs):
    last = lane_id() == 127
    r = [pltpu.roll(x, 127, 1) for x in xs]
    zero = jnp.zeros((8, 128), F32)
    return [jnp.where(last, r[c + 1] if c + 1 < CH else zero, r[c]) for c in range(CH)]


def below_k(xs):
    first = lane_id() == 0
    r = [pltpu.roll(x, 1, 1) for x in xs]
    zero = jnp.zeros((8, 128), F32)
    return [jnp.where(first, r[c - 1] if c else zero, r[c]) for c in range(CH)]


def next_j(xs, edge):
    last = sub_id() == 7
    return [jnp.where(last, edge[c], pltpu.roll(xs[c], 7, 0)) for c in range(CH)]


def below_j(xs, edge):
    first = sub_id() == 0
    return [jnp.where(first, edge[c], pltpu.roll(xs[c], 1, 0)) for c in range(CH)]


def packed_next_k(x):
    r = pltpu.roll(x, 127, 1)
    up = jnp.where((sub_id() & 3) == 3, 0.0, pltpu.roll(r, 7, 0))
    return jnp.where(lane_id() == 127, up, r)


def packed_below_k(x):
    r = pltpu.roll(x, 1, 1)
    down = jnp.where((sub_id() & 3) == 0, 0.0, pltpu.roll(r, 1, 0))
    return jnp.where(lane_id() == 0, down, r)


def at_plane(i, c):
    if isinstance(i, int):
        return pl.ds(i * PR + c * 8, 8)
    return pl.ds(pl.multiple_of(i * PR + c * 8, 8), 8)


def plane(ref, i):
    return [ref[at_plane(i, c), :] for c in range(CH)]


def put_plane(ref, i, xs):
    for c in range(CH):
        ref[at_plane(i, c), :] = xs[c]


def edge_rows(ref, r):
    return [jnp.broadcast_to(ref[pl.ds(r + c, 1), :], (8, 128)) for c in range(CH)]


def mul(xs, ys):
    return [x * y for x, y in zip(xs, ys)]


def add(xs, ys):
    return [x + y for x, y in zip(xs, ys)]


def sub(xs, ys):
    return [x - y for x, y in zip(xs, ys)]


def total(xs):
    return (xs[0] + xs[1]) + (xs[2] + xs[3])


def weights(vx, vxd, vy, vyd, vz, vzd):
    pos = lambda v: [jnp.maximum(x, 0.0) * COURANT for x in v]
    neg = lambda v: [jnp.minimum(x, 0.0) * -COURANT for x in v]
    out = []
    keep = None
    for v, vd in ((vx, vxd), (vy, vyd), (vz, vzd)):
        up, down = neg(v), pos(vd)
        leave = add(pos(v), neg(vd))
        keep = leave if keep is None else add(keep, leave)
        out += [up, down]
    return [[1.0 - x for x in keep]] + out


def apply_weights(k, c, xu, xd, yu, yd, zu, zd):
    out = []
    for q in range(len(c)):
        s = k[0][q] * c[q] + k[1][q] * xu[q]
        s2 = k[2][q] * xd[q] + k[3][q] * yu[q]
        s3 = k[4][q] * yd[q] + k[5][q] * zu[q]
        out.append((s + s2) + (s3 + k[6][q] * zd[q]))
    return out


def transport_plane(k, field, i, low_ref, high_ref, r):
    c = plane(field, i)
    xu, xd = plane(field, i + 1), plane(field, i - 1)
    yu, yd = next_j(c, edge_rows(high_ref, r)), below_j(c, edge_rows(low_ref, r))
    return apply_weights(k, c, xu, xd, yu, yd, next_k(c), below_k(c))


def pressure_kernel(
    co_h, pv_h, tr_h,
    p_o, vel_o, k_o, c1_o, c1n_o,
    cxe, cy, cz, pxe, py, pz, low_n, e1_send,
    rhs_s, inv_s, a0_s, v_s, vn_send, vn_recv,
    red_send, red_recv,
    pe, pn, vx, vy, vz, vyl, pn0, e5_send, e5_recv, kn, kedge,
    te, t_send, t_r1, t_r2,
    lsem, ssem, rsem, red_ss, red_rs,
):
    w, n = lax.axis_index("wide"), lax.axis_index("narrow")
    has = {
        (1, 0): w < NWIDE - 1, (-1, 0): w > 0, (0, 1): n < NNARROW - 1, (0, -1): n > 0,
    }
    for a in (1, -1):
        for b in (1, -1):
            has[(a, b)] = jnp.logical_and(has[(a, 0)], has[(0, b)])

    loads = [
        pltpu.make_async_copy(src, dst, lsem.at[q])
        for q, (src, dst) in enumerate((
            (co_h.at[1], cy), (pv_h.at[1], py),
            (co_h.at[0], cxe.at[pl.ds(PR, OWN)]), (pv_h.at[0], pxe.at[pl.ds(PR, OWN)]),
            (co_h.at[2], cz), (pv_h.at[2], pz),
            (tr_h, te.at[:, pl.ds(2 * PR, OWN)]),
        ))
    ]
    for copy in loads:
        copy.start()

    y, z = lax.div(w, 8), lax.rem(w, 8)
    group_n = [(w, lax.rem(n + e, 8)) for e in (4, 5, 3, 6, 2, 7, 1)]
    offsets = [(a, b) for a in range(4) for b in range(8) if (a, b) != (0, 0)]
    offsets.sort(key=lambda o: -(min(o[0], 4 - o[0]) + min(o[1], 8 - o[1])))
    group_w = [(lax.rem(y + a, 4) * 8 + lax.rem(z + b, 8), n) for a, b in offsets]
    diagonal = [
        (lax.rem(w + a + NWIDE, NWIDE), lax.rem(n + b + NNARROW, NNARROW)) for a in (1, -1) for b in (1, -1)
    ]
    peers = group_w + group_n + diagonal
    barrier = pltpu.get_barrier_semaphore()
    for a, b in peers:
        pl.semaphore_signal(barrier, inc=1, device_id={"wide": a, "narrow": b}, device_id_type=MESH)

    sent = []
    index = [0]

    def message(src, dst, way):
        q = index[0]
        index[0] += 1
        copy = pltpu.make_async_remote_copy(
            src_ref=src, dst_ref=dst, send_sem=ssem.at[q], recv_sem=rsem.at[q],
            device_id={"wide": w + way[0], "narrow": n + way[1]}, device_id_type=MESH,
        )
        back = (-way[0], -way[1])

        @pl.when(has[way])
        def _():
            copy.start()

        sent.append((copy, way))

        def arrive():
            @pl.when(has[back])
            def _():
                copy.wait_recv()

        return arrive

    def blank(dst, way):
        @pl.when(jnp.logical_not(has[way]))
        def _():
            dst[...] = jnp.zeros(dst.shape, F32)

    for ref, dst in ((cxe, pl.ds(0, PR)), (pxe, pl.ds(0, PR))):
        blank(ref.at[dst], (-1, 0))
    blank(low_n.at[0], (0, -1))
    blank(low_n.at[1], (0, -1))
    for s in range(3):
        blank(v_s.at[s, pl.ds(0, PR)], (-1, 0))
        blank(v_s.at[s, pl.ds(17 * PR, PR)], (1, 0))
        blank(vn_recv.at[s, 0], (0, -1))
        blank(vn_recv.at[s, 1], (0, 1))
    for ref, low, high in ((vx, 0, 18), (vy, 0, 17), (vz, 0, 17)):
        blank(ref.at[pl.ds(low * PR, PR)], (-1, 0))
        blank(ref.at[pl.ds(high * PR, PR)], (1, 0))
    blank(vyl.at[pl.ds(0, 8)], (-1, 0))
    blank(vyl.at[pl.ds(8 + EDGE, 8)], (1, 0))
    blank(e5_recv.at[0], (0, -1))
    blank(e5_recv.at[1], (0, 1))

    def blank_tracers(t, _):
        blank(te.at[t, pl.ds(0, 2 * PR)], (-1, 0))
        blank(te.at[t, pl.ds(18 * PR, 2 * PR)], (1, 0))
        for side, b in ((0, -1), (1, 1)):
            blank(t_r1.at[side, t, pl.ds(8, EDGE)], (0, b))
            blank(t_r2.at[side, t], (0, b))
            blank(t_r1.at[side, t, pl.ds(0, 8)], (-1, b))
            blank(t_r1.at[side, t, pl.ds(8 + EDGE, 8)], (1, b))
        return 0

    lax.fori_loop(0, TR, blank_tracers, 0)

    pl.semaphore_wait(barrier, len(peers))

    def pack(src, base, j):
        return src[pl.ds(base + j, EDGE, stride=8), :]

    got = [
        message(co_h.at[0, pl.ds(OWN - PR, PR)], cxe.at[pl.ds(0, PR)], (1, 0)),
        message(pv_h.at[0, pl.ds(OWN - PR, PR)], pxe.at[pl.ds(0, PR)], (1, 0)),
    ]
    loads[0].wait()
    e1_send[0] = pack(cy, 0, 7)
    loads[1].wait()
    e1_send[1] = pack(py, 0, 7)
    got.append(message(e1_send, low_n, (0, 1)))

    bulk = []

    def send_bulk(chunk):
        t0 = chunk * PER

        def rows(t, _):
            for slot, j in enumerate((0, 1, 6, 7)):
                t_send[slot, t] = te[t, pl.ds(2 * PR + j, EDGE, stride=8), :]
            return 0

        lax.fori_loop(t0, t0 + PER, rows, 0)
        ts = pl.ds(t0, PER)
        main = pl.ds(8, EDGE)
        bulk.extend([
            message(t_send.at[3, ts], t_r1.at[0, ts, main], (0, 1)),
            message(t_send.at[0, ts], t_r1.at[1, ts, main], (0, -1)),
            message(te.at[ts, pl.ds(16 * PR, 2 * PR)], te.at[ts, pl.ds(0, 2 * PR)], (1, 0)),
            message(te.at[ts, pl.ds(2 * PR, 2 * PR)], te.at[ts, pl.ds(18 * PR, 2 * PR)], (-1, 0)),
            message(t_send.at[2, ts], t_r2.at[0, ts], (0, 1)),
            message(t_send.at[1, ts], t_r2.at[1, ts], (0, -1)),
        ])

    def send_corners():
        low, high = pl.ds(0, 8), pl.ds(8 + EDGE, 8)
        first, last = pl.ds(0, 8), pl.ds(EDGE - 8, 8)
        bulk.extend([
            message(t_send.at[3, :, last], t_r1.at[0, :, low], (1, 1)),
            message(t_send.at[3, :, first], t_r1.at[0, :, high], (-1, 1)),
            message(t_send.at[0, :, last], t_r1.at[1, :, low], (1, -1)),
            message(t_send.at[0, :, first], t_r1.at[1, :, high], (-1, -1)),
        ])

    loads[6].wait()
    send_bulk(0)
    for copy in loads[2:6]:
        copy.wait()
    for arrive in got:
        arrive()

    zero = jnp.zeros((8, 128), F32)

    def start_plane(i, acc):
        cxu, cxd = plane(cxe, i + 1), plane(cxe, i)
        cyu, czu = plane(cy, i), plane(cz, i)
        cyd = below_j(cyu, edge_rows(low_n.at[0], i * CH))
        czd = below_k(czu)
        diag = add(add(add(cxu, cxd), add(cyu, cyd)), add(czu, czd))
        pyu, pzu = plane(py, i), plane(pz, i)
        pyd = below_j(pyu, edge_rows(low_n.at[1], i * CH))
        d = sub(plane(pxe, i + 1), plane(pxe, i))
        d = add(add(d, sub(pyu, pyd)), sub(pzu, below_k(pzu)))
        rhs = [-x for x in d]
        inv = [1.0 / x for x in diag]
        v = mul(rhs, inv)
        put_plane(rhs_s, i, rhs)
        put_plane(inv_s, i, inv)
        put_plane(v_s.at[0], i + 1, v)
        return acc + total(mul(rhs, v))

    b0 = lax.fori_loop(0, PLANES, start_plane, zero)

    def exchange(s):
        v = v_s.at[s]
        for slot, j in ((0, 0), (1, 7)):
            vn_send[s, slot] = pack(v, PR, j)
        return [
            message(v.at[pl.ds(PR * 16, PR)], v.at[pl.ds(0, PR)], (1, 0)),
            message(v.at[pl.ds(PR, PR)], v.at[pl.ds(PR * 17, PR)], (-1, 0)),
            message(vn_send.at[s, 1], vn_recv.at[s, 0], (0, 1)),
            message(vn_send.at[s, 0], vn_recv.at[s, 1], (0, -1)),
        ]

    def image(s, i):
        v_ref = v_s.at[s]
        v = plane(v_ref, i + 1)
        vu, vd = plane(v_ref, i + 2), plane(v_ref, i)
        fx = mul(plane(cxe, i + 1), sub(vu, v))
        fxd = mul(plane(cxe, i), sub(v, vd))
        low, high = edge_rows(vn_recv.at[s, 0], i * CH), edge_rows(vn_recv.at[s, 1], i * CH)
        fy = mul(plane(cy, i), sub(next_j(v, high), v))
        edge = mul(edge_rows(low_n.at[0], i * CH), sub(v, low))
        fyd = below_j(fy, edge)
        fz = mul(plane(cz, i), sub(next_k(v), v))
        a = add(add(sub(fxd, fx), sub(fyd, fy)), sub(below_k(fz), fz))
        return v, a

    got = exchange(0)
    send_bulk(1)
    for arrive in got:
        arrive()

    def first_plane(i, acc):
        v, a = image(0, i)
        put_plane(a0_s, i, a)
        new = sub(mul(a, plane(inv_s, i)), [x * SHIFT for x in v])
        put_plane(v_s.at[1], i + 1, new)
        g00, g01, b1 = acc
        return g00 + total(mul(v, a)), g01 + total(mul(new, a)), b1 + total(mul(new, plane(rhs_s, i)))

    g00, g01, b1 = lax.fori_loop(0, PLANES, first_plane, (zero, zero, zero))
    got = exchange(1)
    send_bulk(2)
    for arrive in got:
        arrive()

    def second_plane(i, acc):
        v, a = image(1, i)
        new = sub(mul(a, plane(inv_s, i)), [x * SHIFT for x in v])
        put_plane(v_s.at[2], i + 1, new)
        g11, g12, g02, b2 = acc
        return (
            g11 + total(mul(v, a)), g12 + total(mul(new, a)),
            g02 + total(mul(new, plane(a0_s, i))), b2 + total(mul(new, plane(rhs_s, i))),
        )

    g11, g12, g02, b2 = lax.fori_loop(0, PLANES, second_plane, (zero,) * 4)
    got = exchange(2)
    send_bulk(3)

    lane = lax.broadcasted_iota(jnp.int32, (1, 128), 1)

    def place(x, m):
        s = jnp.sum(jnp.sum(x, axis=0, keepdims=True), axis=1, keepdims=True)
        return jnp.where(lane == m, s, 0.0)

    sums = jnp.zeros((1, 128), F32)
    for m, x in enumerate((b0, b1, b2, g00, g01, g02, g11, g12)):
        sums = sums + place(x, m)
    for arrive in got:
        arrive()

    def third_plane(i, g22):
        v, a = image(2, i)
        return g22 + total(mul(v, a))

    sums = sums + place(lax.fori_loop(0, PLANES, third_plane, zero), 8)

    pending = []
    for g, group in enumerate((group_n, group_w)):
        red_send[g] = sums
        copies = []
        for q, (a, b) in enumerate(group):
            copy = pltpu.make_async_remote_copy(
                src_ref=red_send.at[g], dst_ref=red_recv.at[g, q],
                send_sem=red_ss.at[g, q], recv_sem=red_rs.at[g, q],
                device_id={"wide": a, "narrow": b}, device_id_type=MESH,
            )
            copy.start()
            copies.append(copy)
        if g == 0:
            send_corners()
        for copy in copies:
            copy.wait_recv()
        sums = sums + jnp.sum(red_recv[g, 0 : len(group)], axis=0)
        pending += copies

    b0, b1, b2, g00, g01, g02, g11, g12, g22 = [sums[:, m : m + 1] for m in range(9)]
    ratio = lambda a, b: jnp.where(b > 0.0, a / b, 0.0)
    l1 = g01 / g00
    l2 = g02 / g00
    d1 = g11 - l1 * g01
    t = g12 - l2 * g01
    l3 = ratio(t, d1)
    d2 = g22 - l2 * g02 - l3 * t
    y1 = b1 - l1 * b0
    y2 = b2 - l2 * b0 - l3 * y1
    q2 = ratio(y2, d2)
    q1 = ratio(y1, d1) - l3 * q2
    q0 = b0 / g00 - l1 * q1 - l2 * q2
    q0, q1, q2 = [jnp.broadcast_to(q, (8, 128)) for q in (q0, q1, q2)]

    def combine(i, _):
        vs = [plane(v_s.at[s], i) for s in range(3)]
        put_plane(pe, i, [q0 * vs[0][c] + q1 * vs[1][c] + q2 * vs[2][c] for c in range(CH)])
        return 0

    lax.fori_loop(0, PLANES + 2, combine, 0)
    for side in range(2):
        for r in range(EDGE // 8):
            rows = pl.ds(r * 8, 8)
            pn[side, rows] = (
                q0 * vn_recv[0, side, rows] + q1 * vn_recv[1, side, rows] + q2 * vn_recv[2, side, rows]
            )

    def low_x():
        p0, p1 = plane(pe, 0), plane(pe, 1)
        put_plane(vx, 1, sub(plane(pxe, 0), mul(plane(cxe, 0), sub(p1, p0))))

    low_x()
    vyl[pl.ds(8, EDGE), :] = low_n[1] - low_n[0] * (pack(pe, PR, 0) - pn[0])

    def velocity_plane(i, _):
        p = plane(pe, i + 1)
        put_plane(p_o, i, p)
        ux = sub(plane(pxe, i + 1), mul(plane(cxe, i + 1), sub(plane(pe, i + 2), p)))
        uy = sub(plane(py, i), mul(plane(cy, i), sub(next_j(p, edge_rows(pn.at[1], i * CH)), p)))
        uz = sub(plane(pz, i), mul(plane(cz, i), sub(next_k(p), p)))
        for d, u in enumerate((ux, uy, uz)):
            put_plane(vel_o.at[d], i, u)
        put_plane(vx, i + 2, ux)
        put_plane(vy, i + 1, uy)
        put_plane(vz, i + 1, uz)
        return 0

    lax.fori_loop(0, PLANES, velocity_plane, 0)

    one = lambda i: pl.ds(i * PR, PR)
    got = [
        message(vx.at[one(16)], vx.at[one(0)], (1, 0)),
        message(vx.at[one(2)], vx.at[one(18)], (-1, 0)),
        message(vy.at[one(16)], vy.at[one(0)], (1, 0)),
        message(vy.at[one(1)], vy.at[one(17)], (-1, 0)),
        message(vz.at[one(16)], vz.at[one(0)], (1, 0)),
        message(vz.at[one(1)], vz.at[one(17)], (-1, 0)),
        message(vyl.at[pl.ds(EDGE, 8)], vyl.at[pl.ds(0, 8)], (1, 0)),
        message(vyl.at[pl.ds(8, 8)], vyl.at[pl.ds(8 + EDGE, 8)], (-1, 0)),
    ]
    for slot, j in ((0, 0), (1, 7)):
        e5_send[slot, pl.ds(0, EDGE)] = pack(vy, PR, 0 if slot == 0 else 6)
        e5_send[slot, pl.ds(EDGE, 8)] = zero
        e5_send[slot, pl.ds(EDGE + 4, 4)] = vx[pl.ds(PR + j, CH, stride=8), :]
        e5_send[slot, pl.ds(EDGE + 8, EDGE)] = pack(vx, 2 * PR, j)
        e5_send[slot, pl.ds(2 * EDGE + 8, EDGE)] = pack(vz, PR, j)
    got.append(message(e5_send.at[1], e5_recv.at[0], (0, 1)))
    got.append(message(e5_send.at[0], e5_recv.at[1], (0, -1)))

    for arrive in bulk:
        arrive()

    def plane_weights(i):
        uy, uz = plane(vy, i + 1), plane(vz, i + 1)
        uyd = below_j(uy, edge_rows(vyl, 8 + i * CH))
        return weights(plane(vx, i + 2), plane(vx, i + 1), uy, uyd, uz, below_k(uz))

    def step_plane(i, k):
        for t in range(TR):
            out = transport_plane(k, te.at[t], i + 2, t_r1.at[0, t], t_r1.at[1, t], 8 + i * CH)
            put_plane(c1_o.at[t], i + 1, out)

    def own_plane(i, _):
        k = plane_weights(i)
        for m in range(7):
            put_plane(k_o.at[m], i, k[m])
        step_plane(i, k)
        return 0

    lax.fori_loop(0, PLANES, own_plane, 0)
    for arrive in got:
        arrive()

    for i, way in ((-1, (-1, 0)), (PLANES, (1, 0))):
        inside = jnp.where(has[way], 1.0, 0.0)
        k = [[x * inside for x in m] for m in plane_weights(i)]
        step_plane(i, k)

    kedge[0] = pack(vy, PR, 7)
    for side, way in ((0, (0, -1)), (1, (0, 1))):
        inside = jnp.where(has[way], 1.0, 0.0)
        for r in range(EDGE // 8):
            ev = e5_recv.at[side]
            far = ev[pl.ds(r * 8, 8), :]
            ux, uxd = ev[pl.ds(EDGE + 8 + r * 8, 8), :], ev[pl.ds(EDGE + 4 + r * 8, 8), :]
            uz = ev[pl.ds(2 * EDGE + 8 + r * 8, 8), :]
            if side == 0:
                uy, uyd = vyl[pl.ds(8 + r * 8, 8), :], far
            else:
                uy, uyd = far, kedge[0, pl.ds(r * 8, 8), :]
            k = weights([ux], [uxd], [uy], [uyd], [uz], [packed_below_k(uz)])
            k = [[m[0] * inside] for m in k]

            def row_step(t, _, side=side, r=r, k=k):
                ref = t_r1.at[side, t]
                c = ref[pl.ds(8 + r * 8, 8), :]
                xu, xd = ref[pl.ds(12 + r * 8, 8), :], ref[pl.ds(4 + r * 8, 8), :]
                far = t_r2[side, t, pl.ds(r * 8, 8), :]
                near = t_send[0 if side == 0 else 3, t, pl.ds(r * 8, 8), :]
                yu, yd = (near, far) if side == 0 else (far, near)
                out = apply_weights(k, [c], [xu], [xd], [yu], [yd], [packed_next_k(c)], [packed_below_k(c)])
                c1n_o[side, t, pl.ds(r * 8, 8), :] = out[0]
                return 0

            lax.fori_loop(0, TR, row_step, 0, unroll=8)

    for copy in pending:
        copy.wait_send()
    for copy, way in sent:
        @pl.when(has[way])
        def _(copy=copy):
            copy.wait_send()


def transport_kernel(k_ref, c1, c1n, p, vel, p_h, vel_h, tr_h, out, sem):
    first = [pltpu.make_async_copy(p, p_h, sem.at[0]), pltpu.make_async_copy(vel, vel_h, sem.at[1])]
    for copy in first:
        copy.start()
    copies = []
    parts = 4
    for part in range(parts):

        def own_plane(i, _):
            k = [plane(k_ref.at[m], i) for m in range(7)]
            for t in range(TR):
                put_plane(out.at[t], i, transport_plane(k, c1.at[t], i + 1, c1n.at[0, t], c1n.at[1, t], i * CH))
            return 0

        each = PLANES // parts
        lax.fori_loop(part * each, (part + 1) * each, own_plane, 0)
        rows = pl.ds(part * each * PR, each * PR)
        copy = pltpu.make_async_copy(out.at[:, rows], tr_h.at[:, rows], sem.at[2 + part])
        copy.start()
        copies.append(copy)
    for copy in first + copies:
        copy.wait()


def view(x):
    lead = x.shape[:-3]
    x = x.reshape(x.shape[:-1] + (CH, 128)).swapaxes(-3, -2)
    return x.reshape(lead + (OWN, 128))


def unview(x):
    lead = x.shape[:-2]
    x = x.reshape(lead + (PLANES, CH, 8, 128)).swapaxes(-3, -2)
    return x.reshape(lead + (PLANES, 8, CH * 128))


def body(coefficients, predicted_velocity, tracers):
    shape = lambda *s: jax.ShapeDtypeStruct(s, F32)
    vm = lambda *s: pltpu.VMEM(s, F32)
    hbm = pl.BlockSpec(memory_space=pltpu.HBM)
    vmem = pl.BlockSpec(memory_space=pltpu.VMEM)
    p, vel, k, c1, c1n = pl.pallas_call(
        pressure_kernel,
        out_shape=[
            shape(OWN, 128), shape(3, OWN, 128), shape(7, OWN, 128),
            shape(TR, 18 * PR, 128), shape(2, TR, EDGE, 128),
        ],
        in_specs=[hbm] * 3,
        out_specs=[vmem] * 5,
        scratch_shapes=[
            vm(OWN + PR, 128), vm(OWN, 128), vm(OWN, 128), vm(OWN + PR, 128), vm(OWN, 128), vm(OWN, 128),
            vm(2, EDGE, 128), vm(2, EDGE, 128),
            vm(OWN, 128), vm(OWN, 128), vm(OWN, 128), vm(3, 18 * PR, 128),
            vm(3, 2, EDGE, 128), vm(3, 2, EDGE, 128),
            vm(2, 1, 128), vm(2, 31, 1, 128),
            vm(18 * PR, 128), vm(2, EDGE, 128),
            vm(19 * PR, 128), vm(18 * PR, 128), vm(18 * PR, 128), vm(16 + EDGE, 128), vm(EDGE, 128),
            vm(2, 3 * EDGE + 8, 128), vm(2, 3 * EDGE + 8, 128), vm(7, 8, 128), vm(1, EDGE, 128),
            vm(TR, 20 * PR, 128), vm(4, TR, EDGE, 128), vm(2, TR, 16 + EDGE, 128), vm(2, TR, EDGE, 128),
            pltpu.SemaphoreType.DMA((7,)), pltpu.SemaphoreType.DMA((64,)), pltpu.SemaphoreType.DMA((64,)),
            pltpu.SemaphoreType.DMA((2, 31)), pltpu.SemaphoreType.DMA((2, 31)),
        ],
        compiler_params=pltpu.CompilerParams(
            collective_id=0, has_side_effects=True, vmem_limit_bytes=40 << 20
        ),
    )(view(coefficients), view(predicted_velocity), view(tracers))
    p, vel, tr = pl.pallas_call(
        transport_kernel,
        out_shape=[shape(OWN, 128), shape(3, OWN, 128), shape(TR, OWN, 128)],
        in_specs=[vmem] * 5,
        out_specs=[hbm] * 3,
        scratch_shapes=[vm(TR, OWN, 128), pltpu.SemaphoreType.DMA((6,))],
        compiler_params=pltpu.CompilerParams(vmem_limit_bytes=40 << 20),
    )(k, c1, c1n, p, vel)
    return unview(p), unview(vel), unview(tr)


def solution(mesh):
    placed = (P(None, "wide", "narrow", None),) * 3
    return jax.shard_map(
        body,
        mesh=mesh,
        in_specs=placed,
        out_specs=(P("wide", "narrow", None),) + placed[:2],
        check_vma=False,
    )
```

```python
import functools

import jax
import jax.numpy as jnp
from jax import lax
from jax.experimental import pallas as pl
from jax.experimental.pallas import tpu as pltpu
from jax.sharding import PartitionSpec as P

MESH = pl.DeviceIdType.MESH
F32 = jnp.float32
COURANT = 0.15

PLANES = 16
CH = 4
PR = CH * 8
OWN = PLANES * PR
EDGE = PLANES * CH
TR = 16
CHUNKS = 4
PER = TR // CHUNKS
NWIDE = 32
NNARROW = 8
SHIFT = 1.0


def lane_id():
    return lax.broadcasted_iota(jnp.int32, (8, 128), 1)


def sub_id():
    return lax.broadcasted_iota(jnp.int32, (8, 128), 0)


def next_k(xs):
    last = lane_id() == 127
    r = [pltpu.roll(x, 127, 1) for x in xs]
    zero = jnp.zeros((8, 128), F32)
    return [jnp.where(last, r[c + 1] if c + 1 < CH else zero, r[c]) for c in range(CH)]


def below_k(xs):
    first = lane_id() == 0
    r = [pltpu.roll(x, 1, 1) for x in xs]
    zero = jnp.zeros((8, 128), F32)
    return [jnp.where(first, r[c - 1] if c else zero, r[c]) for c in range(CH)]


def next_j(xs, edge):
    last = sub_id() == 7
    return [jnp.where(last, edge[c], pltpu.roll(xs[c], 7, 0)) for c in range(CH)]


def below_j(xs, edge):
    first = sub_id() == 0
    return [jnp.where(first, edge[c], pltpu.roll(xs[c], 1, 0)) for c in range(CH)]


def packed_next_k(x):
    r = pltpu.roll(x, 127, 1)
    up = jnp.where((sub_id() & 3) == 3, 0.0, pltpu.roll(r, 7, 0))
    return jnp.where(lane_id() == 127, up, r)


def packed_below_k(x):
    r = pltpu.roll(x, 1, 1)
    down = jnp.where((sub_id() & 3) == 0, 0.0, pltpu.roll(r, 1, 0))
    return jnp.where(lane_id() == 0, down, r)


def at_plane(i, c):
    if isinstance(i, int):
        return pl.ds(i * PR + c * 8, 8)
    return pl.ds(pl.multiple_of(i * PR + c * 8, 8), 8)


def plane(ref, i):
    return [ref[at_plane(i, c), :] for c in range(CH)]


def put_plane(ref, i, xs):
    for c in range(CH):
        ref[at_plane(i, c), :] = xs[c]


def edge_rows(ref, r):
    return [jnp.broadcast_to(ref[pl.ds(r + c, 1), :], (8, 128)) for c in range(CH)]


def mul(xs, ys):
    return [x * y for x, y in zip(xs, ys)]


def add(xs, ys):
    return [x + y for x, y in zip(xs, ys)]


def sub(xs, ys):
    return [x - y for x, y in zip(xs, ys)]


def total(xs):
    return (xs[0] + xs[1]) + (xs[2] + xs[3])


def weights(vx, vxd, vy, vyd, vz, vzd):
    pos = lambda v: [jnp.maximum(x, 0.0) * COURANT for x in v]
    neg = lambda v: [jnp.minimum(x, 0.0) * -COURANT for x in v]
    out = []
    keep = None
    for v, vd in ((vx, vxd), (vy, vyd), (vz, vzd)):
        up, down = neg(v), pos(vd)
        leave = add(pos(v), neg(vd))
        keep = leave if keep is None else add(keep, leave)
        out += [up, down]
    return [[1.0 - x for x in keep]] + out


def apply_weights(k, c, xu, xd, yu, yd, zu, zd):
    out = []
    for q in range(len(c)):
        s = k[0][q] * c[q] + k[1][q] * xu[q]
        s2 = k[2][q] * xd[q] + k[3][q] * yu[q]
        s3 = k[4][q] * yd[q] + k[5][q] * zu[q]
        out.append((s + s2) + (s3 + k[6][q] * zd[q]))
    return out


def transport_plane(k, field, i, low_ref, high_ref, r):
    c = plane(field, i)
    xu, xd = plane(field, i + 1), plane(field, i - 1)
    yu, yd = next_j(c, edge_rows(high_ref, r)), below_j(c, edge_rows(low_ref, r))
    return apply_weights(k, c, xu, xd, yu, yd, next_k(c), below_k(c))


def pressure_kernel(
    co_h, pv_h, tr_h,
    p_o, vel_o, k_o, c1_o, c1n_o,
    cxe, cy, cz, pxe, py, pz, low_n, e1_send,
    rhs_s, inv_s, a0_s, v_s, vn_send, vn_recv,
    red_send, red_recv,
    pe, pn, vx, vy, vz, vyl, pn0, e5_send, e5_recv, kn, kedge,
    te, t_send, t_r1, t_r2,
    lsem, ssem, rsem, red_ss, red_rs,
):
    w, n = lax.axis_index("wide"), lax.axis_index("narrow")
    has = {
        (1, 0): w < NWIDE - 1, (-1, 0): w > 0, (0, 1): n < NNARROW - 1, (0, -1): n > 0,
    }
    for a in (1, -1):
        for b in (1, -1):
            has[(a, b)] = jnp.logical_and(has[(a, 0)], has[(0, b)])

    loads = [
        pltpu.make_async_copy(src, dst, lsem.at[q])
        for q, (src, dst) in enumerate((
            (co_h.at[1], cy), (pv_h.at[1], py),
            (co_h.at[0], cxe.at[pl.ds(PR, OWN)]), (pv_h.at[0], pxe.at[pl.ds(PR, OWN)]),
            (co_h.at[2], cz), (pv_h.at[2], pz),
            (tr_h, te.at[:, pl.ds(2 * PR, OWN)]),
        ))
    ]
    for copy in loads:
        copy.start()

    y, z = lax.div(w, 8), lax.rem(w, 8)
    group_n = [(w, lax.rem(n + e, 8)) for e in (4, 5, 3, 6, 2, 7, 1)]
    offsets = [(a, b) for a in range(4) for b in range(8) if (a, b) != (0, 0)]
    offsets.sort(key=lambda o: -(min(o[0], 4 - o[0]) + min(o[1], 8 - o[1])))
    group_w = [(lax.rem(y + a, 4) * 8 + lax.rem(z + b, 8), n) for a, b in offsets]
    diagonal = [
        (lax.rem(w + a + NWIDE, NWIDE), lax.rem(n + b + NNARROW, NNARROW)) for a in (1, -1) for b in (1, -1)
    ]
    peers = group_w + group_n + diagonal
    barrier = pltpu.get_barrier_semaphore()
    for a, b in peers:
        pl.semaphore_signal(barrier, inc=1, device_id={"wide": a, "narrow": b}, device_id_type=MESH)

    sent = []
    index = [0]

    def message(src, dst, way):
        q = index[0]
        index[0] += 1
        copy = pltpu.make_async_remote_copy(
            src_ref=src, dst_ref=dst, send_sem=ssem.at[q], recv_sem=rsem.at[q],
            device_id={"wide": w + way[0], "narrow": n + way[1]}, device_id_type=MESH,
        )
        back = (-way[0], -way[1])

        @pl.when(has[way])
        def _():
            copy.start()

        sent.append((copy, way))

        def arrive():
            @pl.when(has[back])
            def _():
                copy.wait_recv()

        return arrive

    def blank(dst, way):
        @pl.when(jnp.logical_not(has[way]))
        def _():
            dst[...] = jnp.zeros(dst.shape, F32)

    for ref, dst in ((cxe, pl.ds(0, PR)), (pxe, pl.ds(0, PR))):
        blank(ref.at[dst], (-1, 0))
    blank(low_n.at[0], (0, -1))
    blank(low_n.at[1], (0, -1))
    for s in range(3):
        blank(v_s.at[s, pl.ds(0, PR)], (-1, 0))
        blank(v_s.at[s, pl.ds(17 * PR, PR)], (1, 0))
        blank(vn_recv.at[s, 0], (0, -1))
        blank(vn_recv.at[s, 1], (0, 1))
    for ref, low, high in ((vx, 0, 18), (vy, 0, 17), (vz, 0, 17)):
        blank(ref.at[pl.ds(low * PR, PR)], (-1, 0))
        blank(ref.at[pl.ds(high * PR, PR)], (1, 0))
    blank(vyl.at[pl.ds(0, 8)], (-1, 0))
    blank(vyl.at[pl.ds(8 + EDGE, 8)], (1, 0))
    blank(e5_recv.at[0], (0, -1))
    blank(e5_recv.at[1], (0, 1))

    def blank_tracers(t, _):
        blank(te.at[t, pl.ds(0, 2 * PR)], (-1, 0))
        blank(te.at[t, pl.ds(18 * PR, 2 * PR)], (1, 0))
        for side, b in ((0, -1), (1, 1)):
            blank(t_r1.at[side, t, pl.ds(8, EDGE)], (0, b))
            blank(t_r2.at[side, t], (0, b))
            blank(t_r1.at[side, t, pl.ds(0, 8)], (-1, b))
            blank(t_r1.at[side, t, pl.ds(8 + EDGE, 8)], (1, b))
        return 0

    lax.fori_loop(0, TR, blank_tracers, 0)

    pl.semaphore_wait(barrier, len(peers))

    def pack(src, base, j):
        return src[pl.ds(base + j, EDGE, stride=8), :]

    got = [
        message(co_h.at[0, pl.ds(OWN - PR, PR)], cxe.at[pl.ds(0, PR)], (1, 0)),
        message(pv_h.at[0, pl.ds(OWN - PR, PR)], pxe.at[pl.ds(0, PR)], (1, 0)),
    ]
    loads[0].wait()
    e1_send[0] = pack(cy, 0, 7)
    loads[1].wait()
    e1_send[1] = pack(py, 0, 7)
    got.append(message(e1_send, low_n, (0, 1)))

    bulk = []

    def send_bulk(chunk):
        t0 = chunk * PER

        def rows(t, _):
            for slot, j in enumerate((0, 1, 6, 7)):
                t_send[slot, t] = te[t, pl.ds(2 * PR + j, EDGE, stride=8), :]
            return 0

        lax.fori_loop(t0, t0 + PER, rows, 0)
        ts = pl.ds(t0, PER)
        main = pl.ds(8, EDGE)
        bulk.extend([
            message(t_send.at[3, ts], t_r1.at[0, ts, main], (0, 1)),
            message(t_send.at[0, ts], t_r1.at[1, ts, main], (0, -1)),
            message(te.at[ts, pl.ds(16 * PR, 2 * PR)], te.at[ts, pl.ds(0, 2 * PR)], (1, 0)),
            message(te.at[ts, pl.ds(2 * PR, 2 * PR)], te.at[ts, pl.ds(18 * PR, 2 * PR)], (-1, 0)),
            message(t_send.at[2, ts], t_r2.at[0, ts], (0, 1)),
            message(t_send.at[1, ts], t_r2.at[1, ts], (0, -1)),
        ])

    def send_corners():
        low, high = pl.ds(0, 8), pl.ds(8 + EDGE, 8)
        first, last = pl.ds(0, 8), pl.ds(EDGE - 8, 8)
        bulk.extend([
            message(t_send.at[3, :, last], t_r1.at[0, :, low], (1, 1)),
            message(t_send.at[3, :, first], t_r1.at[0, :, high], (-1, 1)),
            message(t_send.at[0, :, last], t_r1.at[1, :, low], (1, -1)),
            message(t_send.at[0, :, first], t_r1.at[1, :, high], (-1, -1)),
        ])

    loads[6].wait()
    send_bulk(0)
    for copy in loads[2:6]:
        copy.wait()
    for arrive in got:
        arrive()

    zero = jnp.zeros((8, 128), F32)

    def start_plane(i, acc):
        cxu, cxd = plane(cxe, i + 1), plane(cxe, i)
        cyu, czu = plane(cy, i), plane(cz, i)
        cyd = below_j(cyu, edge_rows(low_n.at[0], i * CH))
        czd = below_k(czu)
        diag = add(add(add(cxu, cxd), add(cyu, cyd)), add(czu, czd))
        pyu, pzu = plane(py, i), plane(pz, i)
        pyd = below_j(pyu, edge_rows(low_n.at[1], i * CH))
        d = sub(plane(pxe, i + 1), plane(pxe, i))
        d = add(add(d, sub(pyu, pyd)), sub(pzu, below_k(pzu)))
        rhs = [-x for x in d]
        inv = [1.0 / x for x in diag]
        v = mul(rhs, inv)
        put_plane(rhs_s, i, rhs)
        put_plane(inv_s, i, inv)
        put_plane(v_s.at[0], i + 1, v)
        return acc + total(mul(rhs, v))

    b0 = lax.fori_loop(0, PLANES, start_plane, zero, unroll=True)

    def exchange(s):
        v = v_s.at[s]
        for slot, j in ((0, 0), (1, 7)):
            vn_send[s, slot] = pack(v, PR, j)
        return [
            message(v.at[pl.ds(PR * 16, PR)], v.at[pl.ds(0, PR)], (1, 0)),
            message(v.at[pl.ds(PR, PR)], v.at[pl.ds(PR * 17, PR)], (-1, 0)),
            message(vn_send.at[s, 1], vn_recv.at[s, 0], (0, 1)),
            message(vn_send.at[s, 0], vn_recv.at[s, 1], (0, -1)),
        ]

    def image(s, i):
        v_ref = v_s.at[s]
        v = plane(v_ref, i + 1)
        vu, vd = plane(v_ref, i + 2), plane(v_ref, i)
        fx = mul(plane(cxe, i + 1), sub(vu, v))
        fxd = mul(plane(cxe, i), sub(v, vd))
        low, high = edge_rows(vn_recv.at[s, 0], i * CH), edge_rows(vn_recv.at[s, 1], i * CH)
        fy = mul(plane(cy, i), sub(next_j(v, high), v))
        edge = mul(edge_rows(low_n.at[0], i * CH), sub(v, low))
        fyd = below_j(fy, edge)
        fz = mul(plane(cz, i), sub(next_k(v), v))
        a = add(add(sub(fxd, fx), sub(fyd, fy)), sub(below_k(fz), fz))
        return v, a

    got = exchange(0)
    send_bulk(1)
    for arrive in got:
        arrive()

    def first_plane(i, acc):
        v, a = image(0, i)
        put_plane(a0_s, i, a)
        new = sub(mul(a, plane(inv_s, i)), [x * SHIFT for x in v])
        put_plane(v_s.at[1], i + 1, new)
        g00, g01, b1 = acc
        return g00 + total(mul(v, a)), g01 + total(mul(new, a)), b1 + total(mul(new, plane(rhs_s, i)))

    g00, g01, b1 = lax.fori_loop(0, PLANES, first_plane, (zero, zero, zero), unroll=True)
    got = exchange(1)
    send_bulk(2)
    for arrive in got:
        arrive()

    def second_plane(i, acc):
        v, a = image(1, i)
        new = sub(mul(a, plane(inv_s, i)), [x * SHIFT for x in v])
        put_plane(v_s.at[2], i + 1, new)
        g11, g12, g02, b2 = acc
        return (
            g11 + total(mul(v, a)), g12 + total(mul(new, a)),
            g02 + total(mul(new, plane(a0_s, i))), b2 + total(mul(new, plane(rhs_s, i))),
        )

    g11, g12, g02, b2 = lax.fori_loop(0, PLANES, second_plane, (zero,) * 4, unroll=True)
    got = exchange(2)
    send_bulk(3)

    lane = lax.broadcasted_iota(jnp.int32, (1, 128), 1)

    def place(x, m):
        s = jnp.sum(jnp.sum(x, axis=0, keepdims=True), axis=1, keepdims=True)
        return jnp.where(lane == m, s, 0.0)

    sums = jnp.zeros((1, 128), F32)
    for m, x in enumerate((b0, b1, b2, g00, g01, g02, g11, g12)):
        sums = sums + place(x, m)
    for arrive in got:
        arrive()

    def third_plane(i, g22):
        v, a = image(2, i)
        return g22 + total(mul(v, a))

    sums = sums + place(lax.fori_loop(0, PLANES, third_plane, zero, unroll=True), 8)

    pending = []
    for g, group in enumerate((group_n, group_w)):
        red_send[g] = sums
        copies = []
        for q, (a, b) in enumerate(group):
            copy = pltpu.make_async_remote_copy(
                src_ref=red_send.at[g], dst_ref=red_recv.at[g, q],
                send_sem=red_ss.at[g, q], recv_sem=red_rs.at[g, q],
                device_id={"wide": a, "narrow": b}, device_id_type=MESH,
            )
            copy.start()
            copies.append(copy)
        if g == 0:
            send_corners()
        for copy in copies:
            copy.wait_recv()
        sums = sums + jnp.sum(red_recv[g, 0 : len(group)], axis=0)
        pending += copies

    b0, b1, b2, g00, g01, g02, g11, g12, g22 = [sums[:, m : m + 1] for m in range(9)]
    ratio = lambda a, b: jnp.where(b > 0.0, a / b, 0.0)
    l1 = g01 / g00
    l2 = g02 / g00
    d1 = g11 - l1 * g01
    t = g12 - l2 * g01
    l3 = ratio(t, d1)
    d2 = g22 - l2 * g02 - l3 * t
    y1 = b1 - l1 * b0
    y2 = b2 - l2 * b0 - l3 * y1
    q2 = ratio(y2, d2)
    q1 = ratio(y1, d1) - l3 * q2
    q0 = b0 / g00 - l1 * q1 - l2 * q2
    q0, q1, q2 = [jnp.broadcast_to(q, (8, 128)) for q in (q0, q1, q2)]

    def combine(i, _):
        vs = [plane(v_s.at[s], i) for s in range(3)]
        put_plane(pe, i, [q0 * vs[0][c] + q1 * vs[1][c] + q2 * vs[2][c] for c in range(CH)])
        return 0

    lax.fori_loop(0, PLANES + 2, combine, 0, unroll=True)
    for side in range(2):
        for r in range(EDGE // 8):
            rows = pl.ds(r * 8, 8)
            pn[side, rows] = (
                q0 * vn_recv[0, side, rows] + q1 * vn_recv[1, side, rows] + q2 * vn_recv[2, side, rows]
            )

    def low_x():
        p0, p1 = plane(pe, 0), plane(pe, 1)
        put_plane(vx, 1, sub(plane(pxe, 0), mul(plane(cxe, 0), sub(p1, p0))))

    low_x()
    vyl[pl.ds(8, EDGE), :] = low_n[1] - low_n[0] * (pack(pe, PR, 0) - pn[0])

    def velocity_plane(i, _):
        p = plane(pe, i + 1)
        put_plane(p_o, i, p)
        ux = sub(plane(pxe, i + 1), mul(plane(cxe, i + 1), sub(plane(pe, i + 2), p)))
        uy = sub(plane(py, i), mul(plane(cy, i), sub(next_j(p, edge_rows(pn.at[1], i * CH)), p)))
        uz = sub(plane(pz, i), mul(plane(cz, i), sub(next_k(p), p)))
        for d, u in enumerate((ux, uy, uz)):
            put_plane(vel_o.at[d], i, u)
        put_plane(vx, i + 2, ux)
        put_plane(vy, i + 1, uy)
        put_plane(vz, i + 1, uz)
        return 0

    lax.fori_loop(0, PLANES, velocity_plane, 0, unroll=True)

    one = lambda i: pl.ds(i * PR, PR)
    got = [
        message(vx.at[one(16)], vx.at[one(0)], (1, 0)),
        message(vx.at[one(2)], vx.at[one(18)], (-1, 0)),
        message(vy.at[one(16)], vy.at[one(0)], (1, 0)),
        message(vy.at[one(1)], vy.at[one(17)], (-1, 0)),
        message(vz.at[one(16)], vz.at[one(0)], (1, 0)),
        message(vz.at[one(1)], vz.at[one(17)], (-1, 0)),
        message(vyl.at[pl.ds(EDGE, 8)], vyl.at[pl.ds(0, 8)], (1, 0)),
        message(vyl.at[pl.ds(8, 8)], vyl.at[pl.ds(8 + EDGE, 8)], (-1, 0)),
    ]
    for slot, j in ((0, 0), (1, 7)):
        e5_send[slot, pl.ds(0, EDGE)] = pack(vy, PR, 0 if slot == 0 else 6)
        e5_send[slot, pl.ds(EDGE, 8)] = zero
        e5_send[slot, pl.ds(EDGE + 4, 4)] = vx[pl.ds(PR + j, CH, stride=8), :]
        e5_send[slot, pl.ds(EDGE + 8, EDGE)] = pack(vx, 2 * PR, j)
        e5_send[slot, pl.ds(2 * EDGE + 8, EDGE)] = pack(vz, PR, j)
    got.append(message(e5_send.at[1], e5_recv.at[0], (0, 1)))
    got.append(message(e5_send.at[0], e5_recv.at[1], (0, -1)))

    for arrive in bulk:
        arrive()

    def plane_weights(i):
        uy, uz = plane(vy, i + 1), plane(vz, i + 1)
        uyd = below_j(uy, edge_rows(vyl, 8 + i * CH))
        return weights(plane(vx, i + 2), plane(vx, i + 1), uy, uyd, uz, below_k(uz))

    def step_plane(i, k):
        for t in range(TR):
            out = transport_plane(k, te.at[t], i + 2, t_r1.at[0, t], t_r1.at[1, t], 8 + i * CH)
            put_plane(c1_o.at[t], i + 1, out)

    def own_plane(i, _):
        k = plane_weights(i)
        for m in range(7):
            put_plane(k_o.at[m], i, k[m])
        step_plane(i, k)
        return 0

    lax.fori_loop(0, PLANES, own_plane, 0)
    for arrive in got:
        arrive()

    for i, way in ((-1, (-1, 0)), (PLANES, (1, 0))):
        inside = jnp.where(has[way], 1.0, 0.0)
        k = [[x * inside for x in m] for m in plane_weights(i)]
        step_plane(i, k)

    kedge[0] = pack(vy, PR, 7)
    for side, way in ((0, (0, -1)), (1, (0, 1))):
        inside = jnp.where(has[way], 1.0, 0.0)
        for r in range(EDGE // 8):
            ev = e5_recv.at[side]
            far = ev[pl.ds(r * 8, 8), :]
            ux, uxd = ev[pl.ds(EDGE + 8 + r * 8, 8), :], ev[pl.ds(EDGE + 4 + r * 8, 8), :]
            uz = ev[pl.ds(2 * EDGE + 8 + r * 8, 8), :]
            if side == 0:
                uy, uyd = vyl[pl.ds(8 + r * 8, 8), :], far
            else:
                uy, uyd = far, kedge[0, pl.ds(r * 8, 8), :]
            k = weights([ux], [uxd], [uy], [uyd], [uz], [packed_below_k(uz)])
            for m in range(7):
                kn[side, m, pl.ds(r * 8, 8), :] = k[m][0] * inside

    def row_step(t, _):
        for side in range(2):
            ref = t_r1.at[side, t]
            for r in range(EDGE // 8):
                rows = pl.ds(r * 8, 8)
                c = ref[pl.ds(8 + r * 8, 8), :]
                xu, xd = ref[pl.ds(12 + r * 8, 8), :], ref[pl.ds(4 + r * 8, 8), :]
                far = t_r2[side, t, rows, :]
                near = t_send[0 if side == 0 else 3, t, rows, :]
                yu, yd = (near, far) if side == 0 else (far, near)
                k = [[kn[side, m, rows, :]] for m in range(7)]
                out = apply_weights(k, [c], [xu], [xd], [yu], [yd], [packed_next_k(c)], [packed_below_k(c)])
                c1n_o[side, t, rows, :] = out[0]
        return 0

    lax.fori_loop(0, TR, row_step, 0, unroll=2)

    for copy in pending:
        copy.wait_send()
    for copy, way in sent:
        @pl.when(has[way])
        def _(copy=copy):
            copy.wait_send()


def transport_kernel(k_ref, c1, c1n, p, vel, p_h, vel_h, tr_h, out, sem):
    first = [pltpu.make_async_copy(p, p_h, sem.at[0]), pltpu.make_async_copy(vel, vel_h, sem.at[1])]
    for copy in first:
        copy.start()
    copies = []
    parts = 4
    for part in range(parts):

        def own_plane(i, _):
            k = [plane(k_ref.at[m], i) for m in range(7)]
            for t in range(TR):
                put_plane(out.at[t], i, transport_plane(k, c1.at[t], i + 1, c1n.at[0, t], c1n.at[1, t], i * CH))
            return 0

        each = PLANES // parts
        lax.fori_loop(part * each, (part + 1) * each, own_plane, 0)
        rows = pl.ds(part * each * PR, each * PR)
        copy = pltpu.make_async_copy(out.at[:, rows], tr_h.at[:, rows], sem.at[2 + part])
        copy.start()
        copies.append(copy)
    for copy in first + copies:
        copy.wait()


def view(x):
    lead = x.shape[:-3]
    x = x.reshape(x.shape[:-1] + (CH, 128)).swapaxes(-3, -2)
    return x.reshape(lead + (OWN, 128))


def unview(x):
    lead = x.shape[:-2]
    x = x.reshape(lead + (PLANES, CH, 8, 128)).swapaxes(-3, -2)
    return x.reshape(lead + (PLANES, 8, CH * 128))


def body(coefficients, predicted_velocity, tracers):
    shape = lambda *s: jax.ShapeDtypeStruct(s, F32)
    vm = lambda *s: pltpu.VMEM(s, F32)
    hbm = pl.BlockSpec(memory_space=pltpu.HBM)
    vmem = pl.BlockSpec(memory_space=pltpu.VMEM)
    p, vel, k, c1, c1n = pl.pallas_call(
        pressure_kernel,
        out_shape=[
            shape(OWN, 128), shape(3, OWN, 128), shape(7, OWN, 128),
            shape(TR, 18 * PR, 128), shape(2, TR, EDGE, 128),
        ],
        in_specs=[hbm] * 3,
        out_specs=[vmem] * 5,
        scratch_shapes=[
            vm(OWN + PR, 128), vm(OWN, 128), vm(OWN, 128), vm(OWN + PR, 128), vm(OWN, 128), vm(OWN, 128),
            vm(2, EDGE, 128), vm(2, EDGE, 128),
            vm(OWN, 128), vm(OWN, 128), vm(OWN, 128), vm(3, 18 * PR, 128),
            vm(3, 2, EDGE, 128), vm(3, 2, EDGE, 128),
            vm(2, 1, 128), vm(2, 31, 1, 128),
            vm(18 * PR, 128), vm(2, EDGE, 128),
            vm(19 * PR, 128), vm(18 * PR, 128), vm(18 * PR, 128), vm(16 + EDGE, 128), vm(EDGE, 128),
            vm(2, 3 * EDGE + 8, 128), vm(2, 3 * EDGE + 8, 128), vm(2, 7, EDGE, 128), vm(1, EDGE, 128),
            vm(TR, 20 * PR, 128), vm(4, TR, EDGE, 128), vm(2, TR, 16 + EDGE, 128), vm(2, TR, EDGE, 128),
            pltpu.SemaphoreType.DMA((7,)), pltpu.SemaphoreType.DMA((64,)), pltpu.SemaphoreType.DMA((64,)),
            pltpu.SemaphoreType.DMA((2, 31)), pltpu.SemaphoreType.DMA((2, 31)),
        ],
        compiler_params=pltpu.CompilerParams(
            collective_id=0, has_side_effects=True, vmem_limit_bytes=40 << 20
        ),
    )(*[pltpu.with_memory_space_constraint(view(x), pltpu.HBM) for x in (coefficients, predicted_velocity, tracers)])
    p, vel, tr = pl.pallas_call(
        transport_kernel,
        out_shape=[shape(OWN, 128), shape(3, OWN, 128), shape(TR, OWN, 128)],
        in_specs=[vmem] * 5,
        out_specs=[hbm] * 3,
        scratch_shapes=[vm(TR, OWN, 128), pltpu.SemaphoreType.DMA((6,))],
        compiler_params=pltpu.CompilerParams(vmem_limit_bytes=40 << 20),
    )(k, c1, c1n, p, vel)
    return unview(p), unview(vel), unview(tr)


def solution(mesh):
    placed = (P(None, "wide", "narrow", None),) * 3
    return jax.shard_map(
        body,
        mesh=mesh,
        in_specs=placed,
        out_specs=(P("wide", "narrow", None),) + placed[:2],
        check_vma=False,
    )
```

```python
import functools

import jax
import jax.numpy as jnp
from jax import lax
from jax.experimental import pallas as pl
from jax.experimental.pallas import tpu as pltpu
from jax.sharding import PartitionSpec as P

MESH = pl.DeviceIdType.MESH
F32 = jnp.float32
COURANT = 0.15

PLANES = 16
CH = 4
PR = CH * 8
OWN = PLANES * PR
EDGE = PLANES * CH
TR = 16
CHUNKS = 4
PER = TR // CHUNKS
NWIDE = 32
NNARROW = 8
SHIFT = 1.0
N_PIL, N_CY, N_PY = 2 * EDGE, 2 * EDGE + 8, 3 * EDGE + 8
NROWS = 4 * EDGE + 8
CORNERS = ((1, 1), (-1, 1), (1, -1), (-1, -1))


def lane_id():
    return lax.broadcasted_iota(jnp.int32, (8, 128), 1)


def sub_id():
    return lax.broadcasted_iota(jnp.int32, (8, 128), 0)


def next_k(xs):
    last = lane_id() == 127
    r = [pltpu.roll(x, 127, 1) for x in xs]
    zero = jnp.zeros((8, 128), F32)
    return [jnp.where(last, r[c + 1] if c + 1 < CH else zero, r[c]) for c in range(CH)]


def below_k(xs):
    first = lane_id() == 0
    r = [pltpu.roll(x, 1, 1) for x in xs]
    zero = jnp.zeros((8, 128), F32)
    return [jnp.where(first, r[c - 1] if c else zero, r[c]) for c in range(CH)]


def next_j(xs, edge):
    last = sub_id() == 7
    return [jnp.where(last, edge[c], pltpu.roll(xs[c], 7, 0)) for c in range(CH)]


def below_j(xs, edge):
    first = sub_id() == 0
    return [jnp.where(first, edge[c], pltpu.roll(xs[c], 1, 0)) for c in range(CH)]


def packed_next_k(x):
    r = pltpu.roll(x, 127, 1)
    up = jnp.where((sub_id() & 3) == 3, 0.0, pltpu.roll(r, 7, 0))
    return jnp.where(lane_id() == 127, up, r)


def packed_below_k(x):
    r = pltpu.roll(x, 1, 1)
    down = jnp.where((sub_id() & 3) == 0, 0.0, pltpu.roll(r, 1, 0))
    return jnp.where(lane_id() == 0, down, r)


def at_plane(i, c):
    if isinstance(i, int):
        return pl.ds(i * PR + c * 8, 8)
    return pl.ds(pl.multiple_of(i * PR + c * 8, 8), 8)


def plane(ref, i):
    return [ref[at_plane(i, c), :] for c in range(CH)]


def put_plane(ref, i, xs):
    for c in range(CH):
        ref[at_plane(i, c), :] = xs[c]


def edge_rows(ref, r):
    return [jnp.broadcast_to(ref[pl.ds(r + c, 1), :], (8, 128)) for c in range(CH)]


def mul(xs, ys):
    return [x * y for x, y in zip(xs, ys)]


def add(xs, ys):
    return [x + y for x, y in zip(xs, ys)]


def sub(xs, ys):
    return [x - y for x, y in zip(xs, ys)]


def total(xs):
    return (xs[0] + xs[1]) + (xs[2] + xs[3])


def weights(vx, vxd, vy, vyd, vz, vzd):
    pos = lambda v: [jnp.maximum(x, 0.0) * COURANT for x in v]
    neg = lambda v: [jnp.minimum(x, 0.0) * -COURANT for x in v]
    out = []
    keep = None
    for v, vd in ((vx, vxd), (vy, vyd), (vz, vzd)):
        up, down = neg(v), pos(vd)
        leave = add(pos(v), neg(vd))
        keep = leave if keep is None else add(keep, leave)
        out += [up, down]
    return [[1.0 - x for x in keep]] + out


def apply_weights(k, c, xu, xd, yu, yd, zu, zd):
    out = []
    for q in range(len(c)):
        s = k[0][q] * c[q] + k[1][q] * xu[q]
        s2 = k[2][q] * xd[q] + k[3][q] * yu[q]
        s3 = k[4][q] * yd[q] + k[5][q] * zu[q]
        out.append((s + s2) + (s3 + k[6][q] * zd[q]))
    return out


def planes_of(field, at, out, to, k_ref, k_at, low_ref, high_ref, r, which):
    xd = plane(field, which[0] + at - 1)
    c = plane(field, which[0] + at)
    for i in which:
        xu = plane(field, i + at + 1)
        k = [plane(k_ref.at[m], i + k_at) for m in range(7)]
        low, high = edge_rows(low_ref, r + i * CH), edge_rows(high_ref, r + i * CH)
        put_plane(
            out, i + to, apply_weights(k, c, xu, xd, next_j(c, high), below_j(c, low), next_k(c), below_k(c))
        )
        xd, c = c, xu


def pressure_kernel(
    co_h, pv_h, tr_h,
    p_o, vel_o, k_o, c1_o, c1n_o,
    cxe, cy, cz, pxe, py, pz, part, w_recv, w_pil_send, w_pil, n_send, n_recv, d_send, d_recv,
    rhs_s, inv_s, w_inv, n_inv, a0_s, a1_s, v_s, vn_send, vn_recv, vc_recv, wb_recv, nb_send, nb_recv,
    red_send, red_recv,
    pe, pn, vx, vy, vz, vyl, pn0, e5_send, e5_recv, kn, kedge, k_s,
    te, t_send, t_r1, t_r2,
    lsem, ssem, rsem, red_ss, red_rs,
):
    w, n = lax.axis_index("wide"), lax.axis_index("narrow")
    has = {
        (1, 0): w < NWIDE - 1, (-1, 0): w > 0, (0, 1): n < NNARROW - 1, (0, -1): n > 0,
    }
    for a in (1, -1):
        for b in (1, -1):
            has[(a, b)] = jnp.logical_and(has[(a, 0)], has[(0, b)])

    loads = [
        pltpu.make_async_copy(src, dst, lsem.at[q])
        for q, (src, dst) in enumerate((
            (co_h.at[1], cy), (pv_h.at[1], py),
            (co_h.at[0], cxe.at[pl.ds(PR, OWN)]), (pv_h.at[0], pxe.at[pl.ds(PR, OWN)]),
            (co_h.at[2], cz), (pv_h.at[2], pz),
            (tr_h, te.at[:, pl.ds(2 * PR, OWN)]),
        ))
    ]
    for copy in loads:
        copy.start()

    y, z = lax.div(w, 8), lax.rem(w, 8)
    group_n = [(w, lax.rem(n + e, 8)) for e in (4, 5, 3, 6, 2, 7, 1)]
    offsets = [(a, b) for a in range(4) for b in range(8) if (a, b) != (0, 0)]
    offsets.sort(key=lambda o: -(min(o[0], 4 - o[0]) + min(o[1], 8 - o[1])))
    group_w = [(lax.rem(y + a, 4) * 8 + lax.rem(z + b, 8), n) for a, b in offsets]
    diagonal = [
        (lax.rem(w + a + NWIDE, NWIDE), lax.rem(n + b + NNARROW, NNARROW)) for a in (1, -1) for b in (1, -1)
    ]
    peers = group_w + group_n + diagonal
    barrier = pltpu.get_barrier_semaphore()
    for a, b in peers:
        pl.semaphore_signal(barrier, inc=1, device_id={"wide": a, "narrow": b}, device_id_type=MESH)

    sent = []
    index = [0]

    def message(src, dst, way):
        q = index[0]
        index[0] += 1
        copy = pltpu.make_async_remote_copy(
            src_ref=src, dst_ref=dst, send_sem=ssem.at[q], recv_sem=rsem.at[q],
            device_id={"wide": w + way[0], "narrow": n + way[1]}, device_id_type=MESH,
        )
        back = (-way[0], -way[1])

        @pl.when(has[way])
        def _():
            copy.start()

        sent.append((copy, way))

        def arrive():
            @pl.when(has[back])
            def _():
                copy.wait_recv()

        return arrive

    def blank(dst, way, value=0.0):
        @pl.when(jnp.logical_not(has[way]))
        def _():
            dst[...] = jnp.full(dst.shape, value, F32)

    low_cy, low_py = n_recv.at[0, pl.ds(N_CY, EDGE)], n_recv.at[0, pl.ds(N_PY, EDGE)]

    for ref, dst in ((cxe, pl.ds(0, PR)), (pxe, pl.ds(0, PR))):
        blank(ref.at[dst], (-1, 0))
    for side, sign in ((0, -1), (1, 1)):
        blank(w_recv.at[side, 0], (sign, 0))
        blank(w_recv.at[side, 1], (sign, 0), 1.0)
        blank(w_pil.at[side], (sign, 0))
        blank(n_recv.at[side], (0, sign))
        blank(n_recv.at[side, pl.ds(EDGE, EDGE)], (0, sign), 1.0)
        blank(v_s.at[1, pl.ds(side * 17 * PR, PR)], (sign, 0))
        blank(vn_recv.at[1, side], (0, sign))
        blank(wb_recv.at[side], (sign, 0))
        blank(nb_recv.at[side], (0, sign))
        blank(e5_recv.at[side], (0, sign))
    for q, way in enumerate(CORNERS):
        blank(d_recv.at[q], way)
        blank(vc_recv.at[q], way)
    for ref, low, high in ((vx, 0, 18), (vy, 0, 17), (vz, 0, 17)):
        blank(ref.at[pl.ds(low * PR, PR)], (-1, 0))
        blank(ref.at[pl.ds(high * PR, PR)], (1, 0))
    blank(vyl.at[pl.ds(0, 8)], (-1, 0))
    blank(vyl.at[pl.ds(8 + EDGE, 8)], (1, 0))

    def blank_tracers(t, _):
        blank(te.at[t, pl.ds(0, 2 * PR)], (-1, 0))
        blank(te.at[t, pl.ds(18 * PR, 2 * PR)], (1, 0))
        for side, b in ((0, -1), (1, 1)):
            blank(t_r1.at[side, t, pl.ds(8, EDGE)], (0, b))
            blank(t_r2.at[side, t], (0, b))
            blank(t_r1.at[side, t, pl.ds(0, 8)], (-1, b))
            blank(t_r1.at[side, t, pl.ds(8 + EDGE, 8)], (1, b))
        return 0

    lax.fori_loop(0, TR, blank_tracers, 0)

    def pack(src, base, j):
        return src[pl.ds(base + j, EDGE, stride=8), :]

    def pillar(src, base, i, j):
        return src[pl.ds(base + i * PR + j, CH, stride=8), :]

    zero = jnp.zeros((8, 128), F32)
    first_j, last_j = sub_id() == 0, sub_id() == 7

    for copy in loads[:6]:
        copy.wait()
    for i in range(PLANES):
        cxu, cyu, czu = plane(cxe, i + 1), plane(cy, i), plane(cz, i)
        diag = add(add(cxu, add(cyu, below_j(cyu, [zero] * CH))), add(czu, below_k(czu)))
        pxu, pyu, pzu = plane(pxe, i + 1), plane(py, i), plane(pz, i)
        d = add(add(pxu, sub(pyu, below_j(pyu, [zero] * CH))), sub(pzu, below_k(pzu)))
        if i:
            diag = add(diag, plane(cxe, i))
            d = sub(d, plane(pxe, i))
        put_plane(part.at[0], i, [-x for x in d])
        put_plane(part.at[1], i, diag)
    for side, i, j in ((0, 0, 0), (1, PLANES - 1, 7)):
        n_send[side, pl.ds(0, EDGE)] = pack(part.at[0], 0, j)
        n_send[side, pl.ds(EDGE, EDGE)] = pack(part.at[1], 0, j)
        n_send[side, pl.ds(N_PIL, 8)] = zero
        n_send[side, pl.ds(N_PIL, CH)] = pillar(cxe, PR, PLANES - 1, j)
        w_pil_send[side] = zero
        w_pil_send[side, pl.ds(0, CH)] = pillar(cy, 0, i, 7)
    n_send[1, pl.ds(N_CY, EDGE)] = pack(cy, 0, 7)
    n_send[1, pl.ds(N_PY, EDGE)] = pack(py, 0, 7)
    for q, (a, b) in enumerate(CORNERS):
        i, j = (PLANES - 1 if a > 0 else 0), (7 if b > 0 else 0)
        for m, (ref, base) in enumerate(((cxe, PR), (pxe, PR), (cy, 0), (py, 0))):
            d_send[q, pl.ds(m * CH, CH)] = pillar(ref, base, i, j)

    pl.semaphore_wait(barrier, len(peers))

    got = [
        message(d_send.at[q], d_recv.at[3 - q], way) for q, way in enumerate(CORNERS) if way != (-1, -1)
    ]
    last, front = pl.ds(OWN - PR, PR), pl.ds(0, PR)
    n_low = pl.ds(0, N_CY)
    got += [
        message(part.at[:, last], w_recv.at[0], (1, 0)),
        message(part.at[:, front], w_recv.at[1], (-1, 0)),
        message(n_send.at[1], n_recv.at[0], (0, 1)),
        message(n_send.at[0, n_low], n_recv.at[1, n_low], (0, -1)),
        message(cxe.at[pl.ds(OWN, PR)], cxe.at[front], (1, 0)),
        message(pxe.at[pl.ds(OWN, PR)], pxe.at[front], (1, 0)),
        message(w_pil_send.at[1], w_pil.at[0], (1, 0)),
        message(w_pil_send.at[0], w_pil.at[1], (-1, 0)),
    ]

    bulk = []

    def pack_tracers():
        def rows(t, _):
            for slot, j in enumerate((0, 1, 6, 7)):
                t_send[slot, t] = te[t, pl.ds(2 * PR + j, EDGE, stride=8), :]
            return 0

        lax.fori_loop(0, TR, rows, 0)

    def send_rows(chunk):
        ts, main = pl.ds(chunk * PER, PER), pl.ds(8, EDGE)
        bulk.extend([
            message(t_send.at[3, ts], t_r1.at[0, ts, main], (0, 1)),
            message(t_send.at[0, ts], t_r1.at[1, ts, main], (0, -1)),
            message(t_send.at[2, ts], t_r2.at[0, ts], (0, 1)),
            message(t_send.at[1, ts], t_r2.at[1, ts], (0, -1)),
        ])

    def send_planes(chunk):
        ts = pl.ds(chunk * PER, PER)
        bulk.extend([
            message(te.at[ts, pl.ds(16 * PR, 2 * PR)], te.at[ts, pl.ds(0, 2 * PR)], (1, 0)),
            message(te.at[ts, pl.ds(2 * PR, 2 * PR)], te.at[ts, pl.ds(18 * PR, 2 * PR)], (-1, 0)),
        ])

    def send_corners():
        low, high = pl.ds(0, 8), pl.ds(8 + EDGE, 8)
        first, last = pl.ds(0, 8), pl.ds(EDGE - 8, 8)
        bulk.extend([
            message(t_send.at[3, :, last], t_r1.at[0, :, low], (1, 1)),
            message(t_send.at[3, :, first], t_r1.at[0, :, high], (-1, 1)),
            message(t_send.at[0, :, last], t_r1.at[1, :, low], (1, -1)),
            message(t_send.at[0, :, first], t_r1.at[1, :, high], (-1, -1)),
        ])

    loads[6].wait()
    pack_tracers()
    send_rows(0)
    send_rows(1)
    send_planes(0)
    send_planes(1)
    for arrive in got:
        arrive()

    corner = {way: d_recv.at[q] for q, way in enumerate(CORNERS)}
    pick_low = lambda rows: [jnp.where(first_j, x, 0.0) for x in rows]
    pick_high = lambda rows: [jnp.where(last_j, x, 0.0) for x in rows]

    b0 = zero
    for i in range(PLANES):
        rhs = add(plane(part.at[0], i), pick_low(edge_rows(low_py, i * CH)))
        diag = add(plane(part.at[1], i), pick_low(edge_rows(low_cy, i * CH)))
        if i == 0:
            rhs, diag = add(rhs, plane(pxe, 0)), add(diag, plane(cxe, 0))
        inv = [1.0 / x for x in diag]
        v = mul(rhs, inv)
        put_plane(rhs_s, i, rhs)
        put_plane(inv_s, i, inv)
        put_plane(v_s.at[0], i + 1, v)
        b0 = b0 + total(mul(rhs, v))
    for side, sign in ((0, -1), (1, 1)):
        inside = jnp.where(has[(sign, 0)], 1.0, 0.0)
        ref = corner[(sign, -1)]
        rhs = add(plane(w_recv.at[side, 0], 0), pick_low(edge_rows(ref, 3 * CH)))
        diag = add(plane(w_recv.at[side, 1], 0), pick_low(edge_rows(ref, 2 * CH)))
        if side:
            rhs, diag = add(rhs, plane(pxe, PLANES)), add(diag, plane(cxe, PLANES))
        inv = [inside / x for x in diag]
        put_plane(w_inv.at[side], 0, inv)
        put_plane(v_s.at[0], 17 * side, mul(rhs, inv))
    for side, sign in ((0, -1), (1, 1)):
        inside = jnp.where(has[(0, sign)], 1.0, 0.0)
        ref = corner[(-1, sign)]
        head, mid = pl.ds(0, CH), pl.ds(EDGE, CH)
        n_recv[side, head] = n_recv[side, head] + ref[pl.ds(CH, CH), :]
        n_recv[side, mid] = n_recv[side, mid] + ref[pl.ds(0, CH), :]
        rhs, diag = n_recv[side, pl.ds(0, EDGE)], n_recv[side, pl.ds(EDGE, EDGE)]
        if side:
            rhs, diag = rhs + n_send[1, pl.ds(N_PY, EDGE)], diag + n_send[1, pl.ds(N_CY, EDGE)]
        inv = inside / diag
        n_inv[side] = inv
        vn_recv[0, side] = rhs * inv

    def image(s, i):
        v_ref = v_s.at[s]
        v = plane(v_ref, i + 1)
        vu, vd = plane(v_ref, i + 2), plane(v_ref, i)
        fx = mul(plane(cxe, i + 1), sub(vu, v))
        fxd = mul(plane(cxe, i), sub(v, vd))
        low, high = edge_rows(vn_recv.at[s, 0], i * CH), edge_rows(vn_recv.at[s, 1], i * CH)
        fy = mul(plane(cy, i), sub(next_j(v, high), v))
        edge = mul(edge_rows(low_cy, i * CH), sub(v, low))
        fyd = below_j(fy, edge)
        fz = mul(plane(cz, i), sub(next_k(v), v))
        a = add(add(sub(fxd, fx), sub(fyd, fy)), sub(below_k(fz), fz))
        return v, a

    g00 = g01 = b1 = zero
    for i in range(PLANES):
        v, a = image(0, i)
        put_plane(a0_s, i, a)
        new = sub(mul(a, plane(inv_s, i)), [x * SHIFT for x in v])
        put_plane(v_s.at[1], i + 1, new)
        g00, g01, b1 = g00 + total(mul(v, a)), g01 + total(mul(new, a)), b1 + total(mul(new, plane(rhs_s, i)))

    v1 = v_s.at[1]
    for slot, j in ((0, 0), (1, 7)):
        vn_send[1, slot] = pack(v1, PR, j)
    got = [
        message(vn_send.at[1, 1 if b > 0 else 0, pl.ds(EDGE - 8 if a > 0 else 0, 8)], vc_recv.at[3 - q], (a, b))
        for q, (a, b) in enumerate(CORNERS)
    ]
    got += [
        message(v1.at[pl.ds(PR * 16, PR)], v1.at[pl.ds(0, PR)], (1, 0)),
        message(v1.at[pl.ds(PR, PR)], v1.at[pl.ds(PR * 17, PR)], (-1, 0)),
        message(vn_send.at[1, 1], vn_recv.at[1, 0], (0, 1)),
        message(vn_send.at[1, 0], vn_recv.at[1, 1], (0, -1)),
    ]
    fxd = None
    for i in range(PLANES):
        v = plane(v1, i + 1)
        fy = [jnp.where(last_j, 0.0, x) for x in mul(plane(cy, i), sub(next_j(v, v), v))]
        fz = mul(plane(cz, i), sub(next_k(v), v))
        a = add(sub(below_j(fy, [zero] * CH), fy), sub(below_k(fz), fz))
        if i:
            a = add(a, fxd)
        if i < PLANES - 1:
            fxd = mul(plane(cxe, i + 1), sub(plane(v1, i + 2), v))
            a = sub(a, fxd)
        put_plane(a1_s, i, a)
    nb_send[0] = pack(a1_s, 0, 0)
    nb_send[1] = pack(a1_s, 0, 7)
    got += [
        message(a1_s.at[last], wb_recv.at[0], (1, 0)),
        message(a1_s.at[front], wb_recv.at[1], (-1, 0)),
        message(nb_send.at[1], nb_recv.at[0], (0, 1)),
        message(nb_send.at[0], nb_recv.at[1], (0, -1)),
    ]
    send_rows(2)
    send_planes(2)
    send_planes(3)
    send_corners()

    lane = lax.broadcasted_iota(jnp.int32, (1, 128), 1)

    def place(x, m):
        s = jnp.sum(jnp.sum(x, axis=0, keepdims=True), axis=1, keepdims=True)
        return jnp.where(lane == m, s, 0.0)

    sums = jnp.zeros((1, 128), F32)
    for m, x in ((0, b0), (1, b1), (3, g00), (4, g01)):
        sums = sums + place(x, m)
    for arrive in got:
        arrive()

    g11 = g12 = g02 = b2 = zero
    for i in range(PLANES):
        v, a = plane(v1, i + 1), plane(a1_s, i)
        low, high = edge_rows(vn_recv.at[1, 0], i * CH), edge_rows(vn_recv.at[1, 1], i * CH)
        a = add(a, pick_low(mul(edge_rows(low_cy, i * CH), sub(v, low))))
        a = sub(a, pick_high(mul(plane(cy, i), sub(high, v))))
        if i == 0:
            a = add(a, mul(plane(cxe, 0), sub(v, plane(v1, 0))))
        if i == PLANES - 1:
            a = sub(a, mul(plane(cxe, PLANES), sub(plane(v1, PLANES + 1), v)))
        new = sub(mul(a, plane(inv_s, i)), [x * SHIFT for x in v])
        put_plane(v_s.at[2], i + 1, new)
        g11, g12 = g11 + total(mul(v, a)), g12 + total(mul(new, a))
        g02, b2 = g02 + total(mul(new, plane(a0_s, i))), b2 + total(mul(new, plane(rhs_s, i)))

    seen = {way: (vc_recv.at[q], CH if way[0] < 0 else 0) for q, way in enumerate(CORNERS)}
    for side, sign in ((0, -1), (1, 1)):
        v = plane(v1, 17 * side)
        a = plane(wb_recv.at[side], 0)
        if side == 0:
            a = sub(a, mul(plane(cxe, 0), sub(plane(v1, 1), v)))
        else:
            a = add(a, mul(plane(cxe, PLANES), sub(v, plane(v1, PLANES))))
        low, high = edge_rows(*seen[(sign, -1)]), edge_rows(*seen[(sign, 1)])
        a = add(a, pick_low(mul(edge_rows(corner[(sign, -1)], 2 * CH), sub(v, low))))
        a = sub(a, pick_high(mul(edge_rows(w_pil.at[side], 0), sub(high, v))))
        new = sub(mul(a, plane(w_inv.at[side], 0)), [x * SHIFT for x in v])
        put_plane(v_s.at[2], 17 * side, new)
    for side, sign in ((0, -1), (1, 1)):
        head, tail = pl.ds(0, CH), pl.ds(EDGE - CH, CH)
        cell = lambda way: seen[way][0][pl.ds(seen[way][1], CH), :]
        vh, vt = vn_recv[1, side, head], vn_recv[1, side, tail]
        ch, ct = corner[(-1, sign)][pl.ds(0, CH), :], n_recv[side, pl.ds(N_PIL, CH)]
        nb_recv[side, head] = nb_recv[side, head] + ch * (vh - cell((-1, sign)))
        nb_recv[side, tail] = nb_recv[side, tail] - ct * (cell((1, sign)) - vt)
        v, near = vn_recv[1, side], vn_send[1, side]
        if side == 0:
            a = nb_recv[side] - low_cy[...] * (near - v)
        else:
            a = nb_recv[side] + n_send[1, pl.ds(N_CY, EDGE)] * (v - near)
        vn_recv[2, side] = a * n_inv[side] - v * SHIFT

    g22 = zero
    for i in range(PLANES):
        v, a = image(2, i)
        g22 = g22 + total(mul(v, a))
    for m, x in ((2, b2), (5, g02), (6, g11), (7, g12), (8, g22)):
        sums = sums + place(x, m)

    pending = []
    for g, group in enumerate((group_n, group_w)):
        red_send[g] = sums
        copies = []
        for q, (a, b) in enumerate(group):
            copy = pltpu.make_async_remote_copy(
                src_ref=red_send.at[g], dst_ref=red_recv.at[g, q],
                send_sem=red_ss.at[g, q], recv_sem=red_rs.at[g, q],
                device_id={"wide": a, "narrow": b}, device_id_type=MESH,
            )
            copy.start()
            copies.append(copy)
        if g == 1:
            send_rows(3)
        for copy in copies:
            copy.wait_recv()
        sums = sums + jnp.sum(red_recv[g, 0 : len(group)], axis=0)
        pending += copies

    b0, b1, b2, g00, g01, g02, g11, g12, g22 = [sums[:, m : m + 1] for m in range(9)]
    ratio = lambda a, b: jnp.where(b > 0.0, a / b, 0.0)
    l1 = g01 / g00
    l2 = g02 / g00
    d1 = g11 - l1 * g01
    t = g12 - l2 * g01
    l3 = ratio(t, d1)
    d2 = g22 - l2 * g02 - l3 * t
    y1 = b1 - l1 * b0
    y2 = b2 - l2 * b0 - l3 * y1
    q2 = ratio(y2, d2)
    q1 = ratio(y1, d1) - l3 * q2
    q0 = b0 / g00 - l1 * q1 - l2 * q2
    q0, q1, q2 = [jnp.broadcast_to(q, (8, 128)) for q in (q0, q1, q2)]

    def combine(i, _):
        vs = [plane(v_s.at[s], i) for s in range(3)]
        put_plane(pe, i, [q0 * vs[0][c] + q1 * vs[1][c] + q2 * vs[2][c] for c in range(CH)])
        return 0

    lax.fori_loop(0, PLANES + 2, combine, 0, unroll=True)
    for side in range(2):
        for r in range(EDGE // 8):
            rows = pl.ds(r * 8, 8)
            pn[side, rows] = (
                q0 * vn_recv[0, side, rows] + q1 * vn_recv[1, side, rows] + q2 * vn_recv[2, side, rows]
            )

    def low_x():
        p0, p1 = plane(pe, 0), plane(pe, 1)
        put_plane(vx, 1, sub(plane(pxe, 0), mul(plane(cxe, 0), sub(p1, p0))))

    low_x()
    vyl[pl.ds(8, EDGE), :] = low_py[...] - low_cy[...] * (pack(pe, PR, 0) - pn[0])

    def velocity_plane(i, _):
        p = plane(pe, i + 1)
        put_plane(p_o, i, p)
        ux = sub(plane(pxe, i + 1), mul(plane(cxe, i + 1), sub(plane(pe, i + 2), p)))
        uy = sub(plane(py, i), mul(plane(cy, i), sub(next_j(p, edge_rows(pn.at[1], i * CH)), p)))
        uz = sub(plane(pz, i), mul(plane(cz, i), sub(next_k(p), p)))
        for d, u in enumerate((ux, uy, uz)):
            put_plane(vel_o.at[d], i, u)
        put_plane(vx, i + 2, ux)
        put_plane(vy, i + 1, uy)
        put_plane(vz, i + 1, uz)
        return 0

    lax.fori_loop(0, PLANES, velocity_plane, 0, unroll=True)

    one = lambda i: pl.ds(i * PR, PR)
    got = [
        message(vx.at[one(16)], vx.at[one(0)], (1, 0)),
        message(vx.at[one(2)], vx.at[one(18)], (-1, 0)),
        message(vy.at[one(16)], vy.at[one(0)], (1, 0)),
        message(vy.at[one(1)], vy.at[one(17)], (-1, 0)),
        message(vz.at[one(16)], vz.at[one(0)], (1, 0)),
        message(vz.at[one(1)], vz.at[one(17)], (-1, 0)),
        message(vyl.at[pl.ds(EDGE, 8)], vyl.at[pl.ds(0, 8)], (1, 0)),
        message(vyl.at[pl.ds(8, 8)], vyl.at[pl.ds(8 + EDGE, 8)], (-1, 0)),
    ]
    for slot, j in ((0, 0), (1, 7)):
        e5_send[slot, pl.ds(0, EDGE)] = pack(vy, PR, 0 if slot == 0 else 6)
        e5_send[slot, pl.ds(EDGE, 8)] = zero
        e5_send[slot, pl.ds(EDGE + 4, 4)] = vx[pl.ds(PR + j, CH, stride=8), :]
        e5_send[slot, pl.ds(EDGE + 8, EDGE)] = pack(vx, 2 * PR, j)
        e5_send[slot, pl.ds(2 * EDGE + 8, EDGE)] = pack(vz, PR, j)
    got.append(message(e5_send.at[1], e5_recv.at[0], (0, 1)))
    got.append(message(e5_send.at[0], e5_recv.at[1], (0, -1)))

    for arrive in bulk:
        arrive()

    def plane_weights(i):
        uy, uz = plane(vy, i + 1), plane(vz, i + 1)
        uyd = below_j(uy, edge_rows(vyl, 8 + i * CH))
        return weights(plane(vx, i + 2), plane(vx, i + 1), uy, uyd, uz, below_k(uz))

    def put_weights(i, inside=None):
        k = plane_weights(i)
        for m in range(7):
            put_plane(k_s.at[m], i + 1, k[m] if inside is None else [x * inside for x in k[m]])
            if inside is None:
                put_plane(k_o.at[m], i, k[m])

    for i in range(PLANES):
        put_weights(i)

    def own_planes(t, _):
        planes_of(te.at[t], 2, c1_o.at[t], 1, k_s, 1, t_r1.at[0, t], t_r1.at[1, t], 8, range(PLANES))
        return 0

    lax.fori_loop(0, TR, own_planes, 0, unroll=2)
    for arrive in got:
        arrive()

    for i, way in ((-1, (-1, 0)), (PLANES, (1, 0))):
        put_weights(i, jnp.where(has[way], 1.0, 0.0))

    def beside(t, _):
        for i in (-1, PLANES):
            planes_of(te.at[t], 2, c1_o.at[t], 1, k_s, 1, t_r1.at[0, t], t_r1.at[1, t], 8, [i])
        return 0

    lax.fori_loop(0, TR, beside, 0, unroll=4)

    kedge[0] = pack(vy, PR, 7)
    for side, way in ((0, (0, -1)), (1, (0, 1))):
        inside = jnp.where(has[way], 1.0, 0.0)
        for r in range(EDGE // 8):
            ev = e5_recv.at[side]
            far = ev[pl.ds(r * 8, 8), :]
            ux, uxd = ev[pl.ds(EDGE + 8 + r * 8, 8), :], ev[pl.ds(EDGE + 4 + r * 8, 8), :]
            uz = ev[pl.ds(2 * EDGE + 8 + r * 8, 8), :]
            if side == 0:
                uy, uyd = vyl[pl.ds(8 + r * 8, 8), :], far
            else:
                uy, uyd = far, kedge[0, pl.ds(r * 8, 8), :]
            k = weights([ux], [uxd], [uy], [uyd], [uz], [packed_below_k(uz)])
            for m in range(7):
                kn[side, m, pl.ds(r * 8, 8), :] = k[m][0] * inside

    def row_step(t, _):
        for side in range(2):
            ref = t_r1.at[side, t]
            for r in range(EDGE // 8):
                rows = pl.ds(r * 8, 8)
                c = ref[pl.ds(8 + r * 8, 8), :]
                xu, xd = ref[pl.ds(12 + r * 8, 8), :], ref[pl.ds(4 + r * 8, 8), :]
                far = t_r2[side, t, rows, :]
                near = t_send[0 if side == 0 else 3, t, rows, :]
                yu, yd = (near, far) if side == 0 else (far, near)
                k = [[kn[side, m, rows, :]] for m in range(7)]
                out = apply_weights(k, [c], [xu], [xd], [yu], [yd], [packed_next_k(c)], [packed_below_k(c)])
                c1n_o[side, t, rows, :] = out[0]
        return 0

    lax.fori_loop(0, TR, row_step, 0, unroll=2)

    for copy in pending:
        copy.wait_send()
    for copy, way in sent:
        @pl.when(has[way])
        def _(copy=copy):
            copy.wait_send()


def transport_kernel(k_ref, c1, c1n, p, vel, p_h, vel_h, tr_h, out, sem):
    first = [pltpu.make_async_copy(p, p_h, sem.at[0]), pltpu.make_async_copy(vel, vel_h, sem.at[1])]
    for copy in first:
        copy.start()
    copies = [pltpu.make_async_copy(out.at[t], tr_h.at[t], sem.at[2 + t]) for t in range(TR)]
    for t in range(TR):
        planes_of(c1.at[t], 1, out.at[t], 0, k_ref, 0, c1n.at[0, t], c1n.at[1, t], 0, range(PLANES))
        copies[t].start()
    for copy in first + copies:
        copy.wait()


def view(x):
    lead = x.shape[:-3]
    x = x.reshape(x.shape[:-1] + (CH, 128)).swapaxes(-3, -2)
    return x.reshape(lead + (OWN, 128))


def unview(x):
    lead = x.shape[:-2]
    x = x.reshape(lead + (PLANES, CH, 8, 128)).swapaxes(-3, -2)
    return x.reshape(lead + (PLANES, 8, CH * 128))


def body(coefficients, predicted_velocity, tracers):
    shape = lambda *s: jax.ShapeDtypeStruct(s, F32)
    vm = lambda *s: pltpu.VMEM(s, F32)
    hbm = pl.BlockSpec(memory_space=pltpu.HBM)
    vmem = pl.BlockSpec(memory_space=pltpu.VMEM)
    p, vel, k, c1, c1n = pl.pallas_call(
        pressure_kernel,
        out_shape=[
            shape(OWN, 128), shape(3, OWN, 128), shape(7, OWN, 128),
            shape(TR, 18 * PR, 128), shape(2, TR, EDGE, 128),
        ],
        in_specs=[hbm] * 3,
        out_specs=[vmem] * 5,
        scratch_shapes=[
            vm(OWN + PR, 128), vm(OWN, 128), vm(OWN, 128), vm(OWN + PR, 128), vm(OWN, 128), vm(OWN, 128),
            vm(2, OWN, 128), vm(2, 2, PR, 128), vm(2, 8, 128), vm(2, 8, 128),
            vm(2, NROWS, 128), vm(2, NROWS, 128), vm(4, 16, 128), vm(4, 16, 128),
            vm(OWN, 128), vm(OWN, 128), vm(2, PR, 128), vm(2, EDGE, 128), vm(OWN, 128), vm(OWN, 128),
            vm(3, 18 * PR, 128), vm(3, 2, EDGE, 128), vm(3, 2, EDGE, 128), vm(4, 8, 128),
            vm(2, PR, 128), vm(2, EDGE, 128), vm(2, EDGE, 128),
            vm(2, 1, 128), vm(2, 31, 1, 128),
            vm(18 * PR, 128), vm(2, EDGE, 128),
            vm(19 * PR, 128), vm(18 * PR, 128), vm(18 * PR, 128), vm(16 + EDGE, 128), vm(EDGE, 128),
            vm(2, 3 * EDGE + 8, 128), vm(2, 3 * EDGE + 8, 128), vm(2, 7, EDGE, 128), vm(1, EDGE, 128), vm(7, 18 * PR, 128),
            vm(TR, 20 * PR, 128), vm(4, TR, EDGE, 128), vm(2, TR, 16 + EDGE, 128), vm(2, TR, EDGE, 128),
            pltpu.SemaphoreType.DMA((7,)), pltpu.SemaphoreType.DMA((72,)), pltpu.SemaphoreType.DMA((72,)),
            pltpu.SemaphoreType.DMA((2, 31)), pltpu.SemaphoreType.DMA((2, 31)),
        ],
        compiler_params=pltpu.CompilerParams(
            collective_id=0, has_side_effects=True, vmem_limit_bytes=40 << 20
        ),
    )(*[pltpu.with_memory_space_constraint(view(x), pltpu.HBM) for x in (coefficients, predicted_velocity, tracers)])
    p, vel, tr = pl.pallas_call(
        transport_kernel,
        out_shape=[shape(OWN, 128), shape(3, OWN, 128), shape(TR, OWN, 128)],
        in_specs=[vmem] * 5,
        out_specs=[hbm] * 3,
        scratch_shapes=[vm(TR, OWN, 128), pltpu.SemaphoreType.DMA((2 + TR,))],
        compiler_params=pltpu.CompilerParams(vmem_limit_bytes=40 << 20),
    )(k, c1, c1n, p, vel)
    return unview(p), unview(vel), unview(tr)


def solution(mesh):
    placed = (P(None, "wide", "narrow", None),) * 3
    return jax.shard_map(
        body,
        mesh=mesh,
        in_specs=placed,
        out_specs=(P("wide", "narrow", None),) + placed[:2],
        check_vma=False,
    )
```

```python
import functools

import jax
import jax.numpy as jnp
from jax import lax
from jax.experimental import pallas as pl
from jax.experimental.pallas import tpu as pltpu
from jax.sharding import PartitionSpec as P

MESH = pl.DeviceIdType.MESH
F32 = jnp.float32
COURANT = 0.15

PLANES = 16
CH = 4
PR = CH * 8
OWN = PLANES * PR
EDGE = PLANES * CH
TR = 16
CHUNKS = 4
PER = TR // CHUNKS
NWIDE = 32
NNARROW = 8
SHIFT = 1.0
N_PIL, N_CY, N_PY = 2 * EDGE, 2 * EDGE + 8, 3 * EDGE + 8
NROWS = 4 * EDGE + 8
CORNERS = ((1, 1), (-1, 1), (1, -1), (-1, -1))


def lane_id():
    return lax.broadcasted_iota(jnp.int32, (8, 128), 1)


def sub_id():
    return lax.broadcasted_iota(jnp.int32, (8, 128), 0)


def next_k(xs):
    last = lane_id() == 127
    r = [pltpu.roll(x, 127, 1) for x in xs]
    zero = jnp.zeros((8, 128), F32)
    return [jnp.where(last, r[c + 1] if c + 1 < CH else zero, r[c]) for c in range(CH)]


def below_k(xs):
    first = lane_id() == 0
    r = [pltpu.roll(x, 1, 1) for x in xs]
    zero = jnp.zeros((8, 128), F32)
    return [jnp.where(first, r[c - 1] if c else zero, r[c]) for c in range(CH)]


def next_j(xs, edge):
    last = sub_id() == 7
    return [jnp.where(last, edge[c], pltpu.roll(xs[c], 7, 0)) for c in range(CH)]


def below_j(xs, edge):
    first = sub_id() == 0
    return [jnp.where(first, edge[c], pltpu.roll(xs[c], 1, 0)) for c in range(CH)]


def packed_next_k(x):
    r = pltpu.roll(x, 127, 1)
    up = jnp.where((sub_id() & 3) == 3, 0.0, pltpu.roll(r, 7, 0))
    return jnp.where(lane_id() == 127, up, r)


def packed_below_k(x):
    r = pltpu.roll(x, 1, 1)
    down = jnp.where((sub_id() & 3) == 0, 0.0, pltpu.roll(r, 1, 0))
    return jnp.where(lane_id() == 0, down, r)


def at_plane(i, c):
    if isinstance(i, int):
        return pl.ds(i * PR + c * 8, 8)
    return pl.ds(pl.multiple_of(i * PR + c * 8, 8), 8)


def plane(ref, i):
    return [ref[at_plane(i, c), :] for c in range(CH)]


def put_plane(ref, i, xs):
    for c in range(CH):
        ref[at_plane(i, c), :] = xs[c]


def edge_rows(ref, r):
    return [jnp.broadcast_to(ref[pl.ds(r + c, 1), :], (8, 128)) for c in range(CH)]


def mul(xs, ys):
    return [x * y for x, y in zip(xs, ys)]


def add(xs, ys):
    return [x + y for x, y in zip(xs, ys)]


def sub(xs, ys):
    return [x - y for x, y in zip(xs, ys)]


def total(xs):
    return (xs[0] + xs[1]) + (xs[2] + xs[3])


def weights(vx, vxd, vy, vyd, vz, vzd):
    pos = lambda v: [jnp.maximum(x, 0.0) * COURANT for x in v]
    neg = lambda v: [jnp.minimum(x, 0.0) * -COURANT for x in v]
    out = []
    keep = None
    for v, vd in ((vx, vxd), (vy, vyd), (vz, vzd)):
        up, down = neg(v), pos(vd)
        leave = add(pos(v), neg(vd))
        keep = leave if keep is None else add(keep, leave)
        out += [up, down]
    return [[1.0 - x for x in keep]] + out


def apply_weights(k, c, xu, xd, yu, yd, zu, zd):
    out = []
    for q in range(len(c)):
        s = k[0][q] * c[q] + k[1][q] * xu[q]
        s2 = k[2][q] * xd[q] + k[3][q] * yu[q]
        s3 = k[4][q] * yd[q] + k[5][q] * zu[q]
        out.append((s + s2) + (s3 + k[6][q] * zd[q]))
    return out


def planes_of(field, at, out, to, k_ref, k_at, low_ref, high_ref, r, which):
    xd = plane(field, which[0] + at - 1)
    c = plane(field, which[0] + at)
    for i in which:
        xu = plane(field, i + at + 1)
        k = [plane(k_ref.at[m], i + k_at) for m in range(7)]
        low, high = edge_rows(low_ref, r + i * CH), edge_rows(high_ref, r + i * CH)
        put_plane(
            out, i + to, apply_weights(k, c, xu, xd, next_j(c, high), below_j(c, low), next_k(c), below_k(c))
        )
        xd, c = c, xu


def pressure_kernel(
    co_h, pv_h, tr_h,
    p_o, vel_o, k_o, c1_o, c1n_o,
    cxe, cy, cz, pxe, py, pz, part, w_recv, w_pil_send, w_pil, n_send, n_recv, d_send, d_recv,
    rhs_s, inv_s, w_inv, n_inv, a0_s, a1_s, v_s, vn_send, vn_recv, vc_recv, wb_recv, nb_send, nb_recv,
    red_send, red_recv,
    pe, pn, vx, vy, vz, vyl, pn0, e5_send, e5_recv, kn, kedge, k_s,
    te, t_send, t_r1, t_r2,
    lsem, ssem, rsem, red_ss, red_rs,
):
    w, n = lax.axis_index("wide"), lax.axis_index("narrow")
    has = {
        (1, 0): w < NWIDE - 1, (-1, 0): w > 0, (0, 1): n < NNARROW - 1, (0, -1): n > 0,
    }
    for a in (1, -1):
        for b in (1, -1):
            has[(a, b)] = jnp.logical_and(has[(a, 0)], has[(0, b)])

    loads = [
        pltpu.make_async_copy(src, dst, lsem.at[q])
        for q, (src, dst) in enumerate((
            (co_h.at[1], cy), (pv_h.at[1], py),
            (co_h.at[0], cxe.at[pl.ds(PR, OWN)]), (pv_h.at[0], pxe.at[pl.ds(PR, OWN)]),
            (co_h.at[2], cz), (pv_h.at[2], pz),
            (tr_h, te.at[:, pl.ds(2 * PR, OWN)]),
        ))
    ]
    for copy in loads:
        copy.start()

    y, z = lax.div(w, 8), lax.rem(w, 8)
    group_n = [(w, lax.rem(n + e, 8)) for e in (4, 5, 3, 6, 2, 7, 1)]
    offsets = [(a, b) for a in range(4) for b in range(8) if (a, b) != (0, 0)]
    offsets.sort(key=lambda o: -(min(o[0], 4 - o[0]) + min(o[1], 8 - o[1])))
    group_w = [(lax.rem(y + a, 4) * 8 + lax.rem(z + b, 8), n) for a, b in offsets]
    diagonal = [
        (lax.rem(w + a + NWIDE, NWIDE), lax.rem(n + b + NNARROW, NNARROW)) for a in (1, -1) for b in (1, -1)
    ]
    peers = group_w + group_n + diagonal
    barrier = pltpu.get_barrier_semaphore()
    for a, b in peers:
        pl.semaphore_signal(barrier, inc=1, device_id={"wide": a, "narrow": b}, device_id_type=MESH)

    sent = []
    index = [0]

    def message(src, dst, way):
        q = index[0]
        index[0] += 1
        copy = pltpu.make_async_remote_copy(
            src_ref=src, dst_ref=dst, send_sem=ssem.at[q], recv_sem=rsem.at[q],
            device_id={"wide": w + way[0], "narrow": n + way[1]}, device_id_type=MESH,
        )
        back = (-way[0], -way[1])

        @pl.when(has[way])
        def _():
            copy.start()

        sent.append((copy, way))

        def arrive():
            @pl.when(has[back])
            def _():
                copy.wait_recv()

        return arrive

    def blank(dst, way, value=0.0):
        @pl.when(jnp.logical_not(has[way]))
        def _():
            dst[...] = jnp.full(dst.shape, value, F32)

    low_cy, low_py = n_recv.at[0, pl.ds(N_CY, EDGE)], n_recv.at[0, pl.ds(N_PY, EDGE)]

    for ref, dst in ((cxe, pl.ds(0, PR)), (pxe, pl.ds(0, PR))):
        blank(ref.at[dst], (-1, 0))
    for side, sign in ((0, -1), (1, 1)):
        blank(w_recv.at[side, 0], (sign, 0))
        blank(w_recv.at[side, 1], (sign, 0), 1.0)
        blank(w_pil.at[side], (sign, 0))
        blank(n_recv.at[side], (0, sign))
        blank(n_recv.at[side, pl.ds(EDGE, EDGE)], (0, sign), 1.0)
        blank(v_s.at[1, pl.ds(side * 17 * PR, PR)], (sign, 0))
        blank(vn_recv.at[1, side], (0, sign))
        blank(wb_recv.at[side], (sign, 0))
        blank(nb_recv.at[side], (0, sign))
        blank(e5_recv.at[side], (0, sign))
    for q, way in enumerate(CORNERS):
        blank(d_recv.at[q], way)
        blank(vc_recv.at[q], way)
    for ref, low, high in ((vx, 0, 18), (vy, 0, 17), (vz, 0, 17)):
        blank(ref.at[pl.ds(low * PR, PR)], (-1, 0))
        blank(ref.at[pl.ds(high * PR, PR)], (1, 0))
    blank(vyl.at[pl.ds(0, 8)], (-1, 0))
    blank(vyl.at[pl.ds(8 + EDGE, 8)], (1, 0))

    def blank_tracers(t, _):
        blank(te.at[t, pl.ds(0, 2 * PR)], (-1, 0))
        blank(te.at[t, pl.ds(18 * PR, 2 * PR)], (1, 0))
        for side, b in ((0, -1), (1, 1)):
            blank(t_r1.at[side, t, pl.ds(8, EDGE)], (0, b))
            blank(t_r2.at[side, t], (0, b))
            blank(t_r1.at[side, t, pl.ds(0, 8)], (-1, b))
            blank(t_r1.at[side, t, pl.ds(8 + EDGE, 8)], (1, b))
        return 0

    lax.fori_loop(0, TR, blank_tracers, 0)

    def pack(src, base, j):
        return src[pl.ds(base + j, EDGE, stride=8), :]

    def pillar(src, base, i, j):
        return src[pl.ds(base + i * PR + j, CH, stride=8), :]

    zero = jnp.zeros((8, 128), F32)
    first_j, last_j = sub_id() == 0, sub_id() == 7

    for copy in loads[:6]:
        copy.wait()
    for i in range(PLANES):
        cxu, cyu, czu = plane(cxe, i + 1), plane(cy, i), plane(cz, i)
        diag = add(add(cxu, add(cyu, below_j(cyu, [zero] * CH))), add(czu, below_k(czu)))
        pxu, pyu, pzu = plane(pxe, i + 1), plane(py, i), plane(pz, i)
        d = add(add(pxu, sub(pyu, below_j(pyu, [zero] * CH))), sub(pzu, below_k(pzu)))
        if i:
            diag = add(diag, plane(cxe, i))
            d = sub(d, plane(pxe, i))
        put_plane(part.at[0], i, [-x for x in d])
        put_plane(part.at[1], i, diag)
    for side, i, j in ((0, 0, 0), (1, PLANES - 1, 7)):
        n_send[side, pl.ds(0, EDGE)] = pack(part.at[0], 0, j)
        n_send[side, pl.ds(EDGE, EDGE)] = pack(part.at[1], 0, j)
        n_send[side, pl.ds(N_PIL, 8)] = zero
        n_send[side, pl.ds(N_PIL, CH)] = pillar(cxe, PR, PLANES - 1, j)
        w_pil_send[side] = zero
        w_pil_send[side, pl.ds(0, CH)] = pillar(cy, 0, i, 7)
    n_send[1, pl.ds(N_CY, EDGE)] = pack(cy, 0, 7)
    n_send[1, pl.ds(N_PY, EDGE)] = pack(py, 0, 7)
    for q, (a, b) in enumerate(CORNERS):
        i, j = (PLANES - 1 if a > 0 else 0), (7 if b > 0 else 0)
        for m, (ref, base) in enumerate(((cxe, PR), (pxe, PR), (cy, 0), (py, 0))):
            d_send[q, pl.ds(m * CH, CH)] = pillar(ref, base, i, j)

    pl.semaphore_wait(barrier, len(peers))

    got = [
        message(d_send.at[q], d_recv.at[3 - q], way) for q, way in enumerate(CORNERS) if way != (-1, -1)
    ]
    last, front = pl.ds(OWN - PR, PR), pl.ds(0, PR)
    n_low = pl.ds(0, N_CY)
    got += [
        message(part.at[:, last], w_recv.at[0], (1, 0)),
        message(part.at[:, front], w_recv.at[1], (-1, 0)),
        message(n_send.at[1], n_recv.at[0], (0, 1)),
        message(n_send.at[0, n_low], n_recv.at[1, n_low], (0, -1)),
        message(cxe.at[pl.ds(OWN, PR)], cxe.at[front], (1, 0)),
        message(pxe.at[pl.ds(OWN, PR)], pxe.at[front], (1, 0)),
        message(w_pil_send.at[1], w_pil.at[0], (1, 0)),
        message(w_pil_send.at[0], w_pil.at[1], (-1, 0)),
    ]

    bulk = [[] for _ in range(CHUNKS)]
    late = []

    def pack_tracers():
        def rows(t, _):
            for slot, j in enumerate((0, 1, 6, 7)):
                t_send[slot, t] = te[t, pl.ds(2 * PR + j, EDGE, stride=8), :]
            return 0

        lax.fori_loop(0, TR, rows, 0)

    def send_rows(chunk):
        ts, main = pl.ds(chunk * PER, PER), pl.ds(8, EDGE)
        bulk[chunk].extend([
            message(t_send.at[3, ts], t_r1.at[0, ts, main], (0, 1)),
            message(t_send.at[0, ts], t_r1.at[1, ts, main], (0, -1)),
        ])
        late.extend([
            message(t_send.at[2, ts], t_r2.at[0, ts], (0, 1)),
            message(t_send.at[1, ts], t_r2.at[1, ts], (0, -1)),
        ])

    def send_planes(chunk):
        ts = pl.ds(chunk * PER, PER)
        bulk[chunk].extend([
            message(te.at[ts, pl.ds(16 * PR, 2 * PR)], te.at[ts, pl.ds(0, 2 * PR)], (1, 0)),
            message(te.at[ts, pl.ds(2 * PR, 2 * PR)], te.at[ts, pl.ds(18 * PR, 2 * PR)], (-1, 0)),
        ])

    def send_corners():
        low, high = pl.ds(0, 8), pl.ds(8 + EDGE, 8)
        first, last = pl.ds(0, 8), pl.ds(EDGE - 8, 8)
        late.extend([
            message(t_send.at[3, :, last], t_r1.at[0, :, low], (1, 1)),
            message(t_send.at[3, :, first], t_r1.at[0, :, high], (-1, 1)),
            message(t_send.at[0, :, last], t_r1.at[1, :, low], (1, -1)),
            message(t_send.at[0, :, first], t_r1.at[1, :, high], (-1, -1)),
        ])

    loads[6].wait()
    pack_tracers()
    send_rows(0)
    send_rows(1)
    send_planes(0)
    send_planes(1)
    for arrive in got:
        arrive()

    corner = {way: d_recv.at[q] for q, way in enumerate(CORNERS)}
    pick_low = lambda rows: [jnp.where(first_j, x, 0.0) for x in rows]
    pick_high = lambda rows: [jnp.where(last_j, x, 0.0) for x in rows]

    b0 = zero
    for i in range(PLANES):
        rhs = add(plane(part.at[0], i), pick_low(edge_rows(low_py, i * CH)))
        diag = add(plane(part.at[1], i), pick_low(edge_rows(low_cy, i * CH)))
        if i == 0:
            rhs, diag = add(rhs, plane(pxe, 0)), add(diag, plane(cxe, 0))
        inv = [1.0 / x for x in diag]
        v = mul(rhs, inv)
        put_plane(rhs_s, i, rhs)
        put_plane(inv_s, i, inv)
        put_plane(v_s.at[0], i + 1, v)
        b0 = b0 + total(mul(rhs, v))
    for side, sign in ((0, -1), (1, 1)):
        inside = jnp.where(has[(sign, 0)], 1.0, 0.0)
        ref = corner[(sign, -1)]
        rhs = add(plane(w_recv.at[side, 0], 0), pick_low(edge_rows(ref, 3 * CH)))
        diag = add(plane(w_recv.at[side, 1], 0), pick_low(edge_rows(ref, 2 * CH)))
        if side:
            rhs, diag = add(rhs, plane(pxe, PLANES)), add(diag, plane(cxe, PLANES))
        inv = [inside / x for x in diag]
        put_plane(w_inv.at[side], 0, inv)
        put_plane(v_s.at[0], 17 * side, mul(rhs, inv))
    for side, sign in ((0, -1), (1, 1)):
        inside = jnp.where(has[(0, sign)], 1.0, 0.0)
        ref = corner[(-1, sign)]
        head, mid = pl.ds(0, CH), pl.ds(EDGE, CH)
        n_recv[side, head] = n_recv[side, head] + ref[pl.ds(CH, CH), :]
        n_recv[side, mid] = n_recv[side, mid] + ref[pl.ds(0, CH), :]
        rhs, diag = n_recv[side, pl.ds(0, EDGE)], n_recv[side, pl.ds(EDGE, EDGE)]
        if side:
            rhs, diag = rhs + n_send[1, pl.ds(N_PY, EDGE)], diag + n_send[1, pl.ds(N_CY, EDGE)]
        inv = inside / diag
        n_inv[side] = inv
        vn_recv[0, side] = rhs * inv

    def image(s, i):
        v_ref = v_s.at[s]
        v = plane(v_ref, i + 1)
        vu, vd = plane(v_ref, i + 2), plane(v_ref, i)
        fx = mul(plane(cxe, i + 1), sub(vu, v))
        fxd = mul(plane(cxe, i), sub(v, vd))
        low, high = edge_rows(vn_recv.at[s, 0], i * CH), edge_rows(vn_recv.at[s, 1], i * CH)
        fy = mul(plane(cy, i), sub(next_j(v, high), v))
        edge = mul(edge_rows(low_cy, i * CH), sub(v, low))
        fyd = below_j(fy, edge)
        fz = mul(plane(cz, i), sub(next_k(v), v))
        a = add(add(sub(fxd, fx), sub(fyd, fy)), sub(below_k(fz), fz))
        return v, a

    g00 = g01 = b1 = zero
    for i in range(PLANES):
        v, a = image(0, i)
        put_plane(a0_s, i, a)
        new = sub(mul(a, plane(inv_s, i)), [x * SHIFT for x in v])
        put_plane(v_s.at[1], i + 1, new)
        g00, g01, b1 = g00 + total(mul(v, a)), g01 + total(mul(new, a)), b1 + total(mul(new, plane(rhs_s, i)))

    v1 = v_s.at[1]
    for slot, j in ((0, 0), (1, 7)):
        vn_send[1, slot] = pack(v1, PR, j)
    got = [
        message(vn_send.at[1, 1 if b > 0 else 0, pl.ds(EDGE - 8 if a > 0 else 0, 8)], vc_recv.at[3 - q], (a, b))
        for q, (a, b) in enumerate(CORNERS)
    ]
    got += [
        message(v1.at[pl.ds(PR * 16, PR)], v1.at[pl.ds(0, PR)], (1, 0)),
        message(v1.at[pl.ds(PR, PR)], v1.at[pl.ds(PR * 17, PR)], (-1, 0)),
        message(vn_send.at[1, 1], vn_recv.at[1, 0], (0, 1)),
        message(vn_send.at[1, 0], vn_recv.at[1, 1], (0, -1)),
    ]
    fxd = None
    for i in range(PLANES):
        v = plane(v1, i + 1)
        fy = [jnp.where(last_j, 0.0, x) for x in mul(plane(cy, i), sub(next_j(v, v), v))]
        fz = mul(plane(cz, i), sub(next_k(v), v))
        a = add(sub(below_j(fy, [zero] * CH), fy), sub(below_k(fz), fz))
        if i:
            a = add(a, fxd)
        if i < PLANES - 1:
            fxd = mul(plane(cxe, i + 1), sub(plane(v1, i + 2), v))
            a = sub(a, fxd)
        put_plane(a1_s, i, a)
    nb_send[0] = pack(a1_s, 0, 0)
    nb_send[1] = pack(a1_s, 0, 7)
    got += [
        message(a1_s.at[last], wb_recv.at[0], (1, 0)),
        message(a1_s.at[front], wb_recv.at[1], (-1, 0)),
        message(nb_send.at[1], nb_recv.at[0], (0, 1)),
        message(nb_send.at[0], nb_recv.at[1], (0, -1)),
    ]
    send_rows(2)
    send_planes(2)

    lane = lax.broadcasted_iota(jnp.int32, (1, 128), 1)

    def place(x, m):
        s = jnp.sum(jnp.sum(x, axis=0, keepdims=True), axis=1, keepdims=True)
        return jnp.where(lane == m, s, 0.0)

    sums = jnp.zeros((1, 128), F32)
    for m, x in ((0, b0), (1, b1), (3, g00), (4, g01)):
        sums = sums + place(x, m)
    for arrive in got:
        arrive()

    g11 = g12 = g02 = b2 = zero
    for i in range(PLANES):
        v, a = plane(v1, i + 1), plane(a1_s, i)
        low, high = edge_rows(vn_recv.at[1, 0], i * CH), edge_rows(vn_recv.at[1, 1], i * CH)
        a = add(a, pick_low(mul(edge_rows(low_cy, i * CH), sub(v, low))))
        a = sub(a, pick_high(mul(plane(cy, i), sub(high, v))))
        if i == 0:
            a = add(a, mul(plane(cxe, 0), sub(v, plane(v1, 0))))
        if i == PLANES - 1:
            a = sub(a, mul(plane(cxe, PLANES), sub(plane(v1, PLANES + 1), v)))
        new = sub(mul(a, plane(inv_s, i)), [x * SHIFT for x in v])
        put_plane(v_s.at[2], i + 1, new)
        g11, g12 = g11 + total(mul(v, a)), g12 + total(mul(new, a))
        g02, b2 = g02 + total(mul(new, plane(a0_s, i))), b2 + total(mul(new, plane(rhs_s, i)))

    seen = {way: (vc_recv.at[q], CH if way[0] < 0 else 0) for q, way in enumerate(CORNERS)}
    for side, sign in ((0, -1), (1, 1)):
        v = plane(v1, 17 * side)
        a = plane(wb_recv.at[side], 0)
        if side == 0:
            a = sub(a, mul(plane(cxe, 0), sub(plane(v1, 1), v)))
        else:
            a = add(a, mul(plane(cxe, PLANES), sub(v, plane(v1, PLANES))))
        low, high = edge_rows(*seen[(sign, -1)]), edge_rows(*seen[(sign, 1)])
        a = add(a, pick_low(mul(edge_rows(corner[(sign, -1)], 2 * CH), sub(v, low))))
        a = sub(a, pick_high(mul(edge_rows(w_pil.at[side], 0), sub(high, v))))
        new = sub(mul(a, plane(w_inv.at[side], 0)), [x * SHIFT for x in v])
        put_plane(v_s.at[2], 17 * side, new)
    for side, sign in ((0, -1), (1, 1)):
        head, tail = pl.ds(0, CH), pl.ds(EDGE - CH, CH)
        cell = lambda way: seen[way][0][pl.ds(seen[way][1], CH), :]
        vh, vt = vn_recv[1, side, head], vn_recv[1, side, tail]
        ch, ct = corner[(-1, sign)][pl.ds(0, CH), :], n_recv[side, pl.ds(N_PIL, CH)]
        nb_recv[side, head] = nb_recv[side, head] + ch * (vh - cell((-1, sign)))
        nb_recv[side, tail] = nb_recv[side, tail] - ct * (cell((1, sign)) - vt)
        v, near = vn_recv[1, side], vn_send[1, side]
        if side == 0:
            a = nb_recv[side] - low_cy[...] * (near - v)
        else:
            a = nb_recv[side] + n_send[1, pl.ds(N_CY, EDGE)] * (v - near)
        vn_recv[2, side] = a * n_inv[side] - v * SHIFT

    g22 = zero
    for i in range(PLANES):
        v, a = image(2, i)
        g22 = g22 + total(mul(v, a))
    for m, x in ((2, b2), (5, g02), (6, g11), (7, g12), (8, g22)):
        sums = sums + place(x, m)

    pending = []
    for g, group in enumerate((group_n, group_w)):
        red_send[g] = sums
        copies = []
        for q, (a, b) in enumerate(group):
            copy = pltpu.make_async_remote_copy(
                src_ref=red_send.at[g], dst_ref=red_recv.at[g, q],
                send_sem=red_ss.at[g, q], recv_sem=red_rs.at[g, q],
                device_id={"wide": a, "narrow": b}, device_id_type=MESH,
            )
            copy.start()
            copies.append(copy)
        if g == 0:
            pass
        if g == 1:
            send_rows(3)
            send_planes(3)
            send_corners()
        for copy in copies:
            copy.wait_recv()
        sums = sums + jnp.sum(red_recv[g, 0 : len(group)], axis=0)
        pending += copies

    b0, b1, b2, g00, g01, g02, g11, g12, g22 = [sums[:, m : m + 1] for m in range(9)]
    ratio = lambda a, b: jnp.where(b > 0.0, a / b, 0.0)
    l1 = g01 / g00
    l2 = g02 / g00
    d1 = g11 - l1 * g01
    t = g12 - l2 * g01
    l3 = ratio(t, d1)
    d2 = g22 - l2 * g02 - l3 * t
    y1 = b1 - l1 * b0
    y2 = b2 - l2 * b0 - l3 * y1
    q2 = ratio(y2, d2)
    q1 = ratio(y1, d1) - l3 * q2
    q0 = b0 / g00 - l1 * q1 - l2 * q2
    q0, q1, q2 = [jnp.broadcast_to(q, (8, 128)) for q in (q0, q1, q2)]

    def combine(i, _):
        vs = [plane(v_s.at[s], i) for s in range(3)]
        put_plane(pe, i, [q0 * vs[0][c] + q1 * vs[1][c] + q2 * vs[2][c] for c in range(CH)])
        return 0

    lax.fori_loop(0, PLANES + 2, combine, 0, unroll=True)
    for side in range(2):
        for r in range(EDGE // 8):
            rows = pl.ds(r * 8, 8)
            pn[side, rows] = (
                q0 * vn_recv[0, side, rows] + q1 * vn_recv[1, side, rows] + q2 * vn_recv[2, side, rows]
            )

    def low_x():
        p0, p1 = plane(pe, 0), plane(pe, 1)
        put_plane(vx, 1, sub(plane(pxe, 0), mul(plane(cxe, 0), sub(p1, p0))))

    low_x()
    vyl[pl.ds(8, EDGE), :] = low_py[...] - low_cy[...] * (pack(pe, PR, 0) - pn[0])

    def velocity_plane(i, _):
        p = plane(pe, i + 1)
        put_plane(p_o, i, p)
        ux = sub(plane(pxe, i + 1), mul(plane(cxe, i + 1), sub(plane(pe, i + 2), p)))
        uy = sub(plane(py, i), mul(plane(cy, i), sub(next_j(p, edge_rows(pn.at[1], i * CH)), p)))
        uz = sub(plane(pz, i), mul(plane(cz, i), sub(next_k(p), p)))
        for d, u in enumerate((ux, uy, uz)):
            put_plane(vel_o.at[d], i, u)
        put_plane(vx, i + 2, ux)
        put_plane(vy, i + 1, uy)
        put_plane(vz, i + 1, uz)
        return 0

    lax.fori_loop(0, PLANES, velocity_plane, 0, unroll=True)

    one = lambda i: pl.ds(i * PR, PR)
    got = [
        message(vx.at[one(16)], vx.at[one(0)], (1, 0)),
        message(vx.at[one(2)], vx.at[one(18)], (-1, 0)),
        message(vy.at[one(16)], vy.at[one(0)], (1, 0)),
        message(vy.at[one(1)], vy.at[one(17)], (-1, 0)),
        message(vz.at[one(16)], vz.at[one(0)], (1, 0)),
        message(vz.at[one(1)], vz.at[one(17)], (-1, 0)),
        message(vyl.at[pl.ds(EDGE, 8)], vyl.at[pl.ds(0, 8)], (1, 0)),
        message(vyl.at[pl.ds(8, 8)], vyl.at[pl.ds(8 + EDGE, 8)], (-1, 0)),
    ]
    for slot, j in ((0, 0), (1, 7)):
        e5_send[slot, pl.ds(0, EDGE)] = pack(vy, PR, 0 if slot == 0 else 6)
        e5_send[slot, pl.ds(EDGE, 8)] = zero
        e5_send[slot, pl.ds(EDGE + 4, 4)] = vx[pl.ds(PR + j, CH, stride=8), :]
        e5_send[slot, pl.ds(EDGE + 8, EDGE)] = pack(vx, 2 * PR, j)
        e5_send[slot, pl.ds(2 * EDGE + 8, EDGE)] = pack(vz, PR, j)
    got.append(message(e5_send.at[1], e5_recv.at[0], (0, 1)))
    got.append(message(e5_send.at[0], e5_recv.at[1], (0, -1)))

    def plane_weights(i):
        uy, uz = plane(vy, i + 1), plane(vz, i + 1)
        uyd = below_j(uy, edge_rows(vyl, 8 + i * CH))
        return weights(plane(vx, i + 2), plane(vx, i + 1), uy, uyd, uz, below_k(uz))

    def put_weights(i, inside=None):
        k = plane_weights(i)
        for m in range(7):
            put_plane(k_s.at[m], i + 1, k[m] if inside is None else [x * inside for x in k[m]])
            if inside is None:
                put_plane(k_o.at[m], i, k[m])

    for i in range(PLANES):
        put_weights(i)

    def own_planes(t, _):
        planes_of(te.at[t], 2, c1_o.at[t], 1, k_s, 1, t_r1.at[0, t], t_r1.at[1, t], 8, range(PLANES))
        return 0

    for chunk in range(CHUNKS):
        for arrive in bulk[chunk]:
            arrive()
        lax.fori_loop(chunk * PER, (chunk + 1) * PER, own_planes, 0, unroll=2)
    for arrive in late + got:
        arrive()

    for i, way in ((-1, (-1, 0)), (PLANES, (1, 0))):
        put_weights(i, jnp.where(has[way], 1.0, 0.0))

    def beside(t, _):
        for i in (-1, PLANES):
            planes_of(te.at[t], 2, c1_o.at[t], 1, k_s, 1, t_r1.at[0, t], t_r1.at[1, t], 8, [i])
        return 0

    lax.fori_loop(0, TR, beside, 0, unroll=4)

    kedge[0] = pack(vy, PR, 7)
    for side, way in ((0, (0, -1)), (1, (0, 1))):
        inside = jnp.where(has[way], 1.0, 0.0)
        for r in range(EDGE // 8):
            ev = e5_recv.at[side]
            far = ev[pl.ds(r * 8, 8), :]
            ux, uxd = ev[pl.ds(EDGE + 8 + r * 8, 8), :], ev[pl.ds(EDGE + 4 + r * 8, 8), :]
            uz = ev[pl.ds(2 * EDGE + 8 + r * 8, 8), :]
            if side == 0:
                uy, uyd = vyl[pl.ds(8 + r * 8, 8), :], far
            else:
                uy, uyd = far, kedge[0, pl.ds(r * 8, 8), :]
            k = weights([ux], [uxd], [uy], [uyd], [uz], [packed_below_k(uz)])
            for m in range(7):
                kn[side, m, pl.ds(r * 8, 8), :] = k[m][0] * inside

    def row_step(t, _):
        for side in range(2):
            ref = t_r1.at[side, t]
            for r in range(EDGE // 8):
                rows = pl.ds(r * 8, 8)
                c = ref[pl.ds(8 + r * 8, 8), :]
                xu, xd = ref[pl.ds(12 + r * 8, 8), :], ref[pl.ds(4 + r * 8, 8), :]
                far = t_r2[side, t, rows, :]
                near = t_send[0 if side == 0 else 3, t, rows, :]
                yu, yd = (near, far) if side == 0 else (far, near)
                k = [[kn[side, m, rows, :]] for m in range(7)]
                out = apply_weights(k, [c], [xu], [xd], [yu], [yd], [packed_next_k(c)], [packed_below_k(c)])
                c1n_o[side, t, rows, :] = out[0]
        return 0

    lax.fori_loop(0, TR, row_step, 0, unroll=2)

    for copy in pending:
        copy.wait_send()
    for copy, way in sent:
        @pl.when(has[way])
        def _(copy=copy):
            copy.wait_send()


def transport_kernel(k_ref, c1, c1n, p, vel, p_h, vel_h, tr_h, out, sem):
    first = [pltpu.make_async_copy(p, p_h, sem.at[0]), pltpu.make_async_copy(vel, vel_h, sem.at[1])]
    for copy in first:
        copy.start()
    copies = [pltpu.make_async_copy(out.at[t], tr_h.at[t], sem.at[2 + t]) for t in range(TR)]
    for t in range(TR):
        planes_of(c1.at[t], 1, out.at[t], 0, k_ref, 0, c1n.at[0, t], c1n.at[1, t], 0, range(PLANES))
        copies[t].start()
    for copy in first + copies:
        copy.wait()


def view(x):
    lead = x.shape[:-3]
    x = x.reshape(x.shape[:-1] + (CH, 128)).swapaxes(-3, -2)
    return x.reshape(lead + (OWN, 128))


def unview(x):
    lead = x.shape[:-2]
    x = x.reshape(lead + (PLANES, CH, 8, 128)).swapaxes(-3, -2)
    return x.reshape(lead + (PLANES, 8, CH * 128))


def body(coefficients, predicted_velocity, tracers):
    shape = lambda *s: jax.ShapeDtypeStruct(s, F32)
    vm = lambda *s: pltpu.VMEM(s, F32)
    hbm = pl.BlockSpec(memory_space=pltpu.HBM)
    vmem = pl.BlockSpec(memory_space=pltpu.VMEM)
    p, vel, k, c1, c1n = pl.pallas_call(
        pressure_kernel,
        out_shape=[
            shape(OWN, 128), shape(3, OWN, 128), shape(7, OWN, 128),
            shape(TR, 18 * PR, 128), shape(2, TR, EDGE, 128),
        ],
        in_specs=[hbm] * 3,
        out_specs=[vmem] * 5,
        scratch_shapes=[
            vm(OWN + PR, 128), vm(OWN, 128), vm(OWN, 128), vm(OWN + PR, 128), vm(OWN, 128), vm(OWN, 128),
            vm(2, OWN, 128), vm(2, 2, PR, 128), vm(2, 8, 128), vm(2, 8, 128),
            vm(2, NROWS, 128), vm(2, NROWS, 128), vm(4, 16, 128), vm(4, 16, 128),
            vm(OWN, 128), vm(OWN, 128), vm(2, PR, 128), vm(2, EDGE, 128), vm(OWN, 128), vm(OWN, 128),
            vm(3, 18 * PR, 128), vm(3, 2, EDGE, 128), vm(3, 2, EDGE, 128), vm(4, 8, 128),
            vm(2, PR, 128), vm(2, EDGE, 128), vm(2, EDGE, 128),
            vm(2, 1, 128), vm(2, 31, 1, 128),
            vm(18 * PR, 128), vm(2, EDGE, 128),
            vm(19 * PR, 128), vm(18 * PR, 128), vm(18 * PR, 128), vm(16 + EDGE, 128), vm(EDGE, 128),
            vm(2, 3 * EDGE + 8, 128), vm(2, 3 * EDGE + 8, 128), vm(2, 7, EDGE, 128), vm(1, EDGE, 128), vm(7, 18 * PR, 128),
            vm(TR, 20 * PR, 128), vm(4, TR, EDGE, 128), vm(2, TR, 16 + EDGE, 128), vm(2, TR, EDGE, 128),
            pltpu.SemaphoreType.DMA((7,)), pltpu.SemaphoreType.DMA((72,)), pltpu.SemaphoreType.DMA((72,)),
            pltpu.SemaphoreType.DMA((2, 31)), pltpu.SemaphoreType.DMA((2, 31)),
        ],
        compiler_params=pltpu.CompilerParams(
            collective_id=0, has_side_effects=True, vmem_limit_bytes=40 << 20
        ),
    )(*[pltpu.with_memory_space_constraint(view(x), pltpu.HBM) for x in (coefficients, predicted_velocity, tracers)])
    p, vel, tr = pl.pallas_call(
        transport_kernel,
        out_shape=[shape(OWN, 128), shape(3, OWN, 128), shape(TR, OWN, 128)],
        in_specs=[vmem] * 5,
        out_specs=[hbm] * 3,
        scratch_shapes=[vm(TR, OWN, 128), pltpu.SemaphoreType.DMA((2 + TR,))],
        compiler_params=pltpu.CompilerParams(vmem_limit_bytes=40 << 20),
    )(k, c1, c1n, p, vel)
    return unview(p), unview(vel), unview(tr)


def solution(mesh):
    placed = (P(None, "wide", "narrow", None),) * 3
    return jax.shard_map(
        body,
        mesh=mesh,
        in_specs=placed,
        out_specs=(P("wide", "narrow", None),) + placed[:2],
        check_vma=False,
    )
```
